128 devices in a mesh: src: 8 (over y, core), tgt: 16 (over z, x).
Axes of the slice: x: 4, y: 4, z: 4, core: 2. Of those that a mesh axis runs over, the one named last changes fastest.
Arguments:
- node_feats: bfloat16 [131072, 256], P(('src', 'tgt')), may hold values from -6 to 6
- send_block: int32 [128, 128, 2], P(('src', 'tgt')), may hold values from 0 to 7
- recv_block: int32 [128, 128, 2], P(('src', 'tgt')), may hold values from 0 to 7
- recv_rel: int32 [128, 128, 2], P(('src', 'tgt')), may hold values from 0 to 29
- recv_count: int32 [128, 128], P(('src', 'tgt')), may hold values from 0 to 2, as said below
- recv_adj: bfloat16 [128, 128, 2, 128, 128], P(('src', 'tgt')), may hold values from 0.1 to 100, as said below
- local_src: int32 [128, 64], P(('src', 'tgt')), may hold values from 0 to 7
- local_tgt: int32 [128, 64], P(('src', 'tgt')), may hold values from 0 to 7
- local_rel: int32 [128, 64], P(('src', 'tgt')), may hold values from 0 to 29
- local_adj: bfloat16 [128, 64, 128, 128], P(('src', 'tgt')), may hold values from 0.1 to 100, as said below
- bases: bfloat16 [8, 256, 256], replicated, may hold values from -0.375 to 0.375
- coeffs: bfloat16 [30, 8], replicated, may hold values from -2 to 2
- self_weight: bfloat16 [256, 256], replicated, may hold values from -0.375 to 0.375
- cotangent: bfloat16 [131072, 256], P(('src', 'tgt')), may hold values from -6 to 6
Outputs:
- features_out: bfloat16 [131072, 256], P(('src', 'tgt'))
- grad_features: bfloat16 [131072, 256], P(('src', 'tgt'))
- grad_bases: float32 [8, 256, 256], replicated
- grad_coef: float32 [30, 8], replicated
- grad_self: float32 [256, 256], replicated
The draws below stay inside these ranges and needn't reach their ends.
Inputs may be any that keep to these rules, and one draw needn't show every extreme that they name: Only the first recv_count[q, p] slots from band p to band q are valid; in every draw some band takes 2 valid slots from every band. `recv_adj`: positive edge weights. `local_adj`: positive edge weights.
All inputs are finite; a program needn't handle non-finite values.
Results may differ from the reference program's by a relative error of at most 0.0068.
Values may be sent and summed in bfloat16 or wider, within the bound.
A program may use at most 256 MiB of HBM per device.

```python
import math
import jax
import jax.numpy as jnp
from jax import lax

WIDTH = 256
RELATIONS = 30
BASES = 8
BLOCK = 128
SLOTS = 2
BLOCKS_DEV = 8
LOCAL_SLOTS = 64
PEERS = 128
NODES = 131072


def adjacency_scales(key, spread):
    row_key, col_key = jax.random.split(key)
    row_scale = jnp.exp(jax.random.uniform(row_key, (BLOCK,), jnp.float32) * spread)
    col_scale = jnp.exp(jax.random.uniform(col_key, (BLOCK,), jnp.float32) * spread)
    return (row_scale, col_scale)


def weights_from(base_key, shape, row_scale, col_scale):
    uniform_part = jax.random.uniform(base_key, shape, jnp.float32)
    values = (0.1 + 0.9 * uniform_part) * row_scale[:, None] * col_scale[None, :]
    return values.astype(jnp.bfloat16)


def draw_recv_adj(key, part):
    row_scale, col_scale = adjacency_scales(key, math.log(10.0))
    key = jax.random.fold_in(key, 11)
    return weights_from(key, (PEERS, PEERS, SLOTS, BLOCK, BLOCK), row_scale, col_scale)


def draw_local_adj(key, part):
    row_scale, col_scale = adjacency_scales(key, math.log(10.0))
    key = jax.random.fold_in(key, 13)
    return weights_from(key, (PEERS, LOCAL_SLOTS, BLOCK, BLOCK), row_scale, col_scale)


def draw_recv_count(key, part):
    key = jax.random.fold_in(key, 5)
    count_key, row_key = jax.random.split(key)
    counts = jax.random.randint(count_key, (PEERS, PEERS), 0, SLOTS + 1, dtype=jnp.int32)
    full_row = jax.random.randint(row_key, (), 0, PEERS, dtype=jnp.int32)
    row_ids = jnp.arange(PEERS, dtype=jnp.int32)[:, None]
    counts = jnp.where(row_ids == full_row, SLOTS, counts)
    return counts.astype(jnp.int32)


def with_ends(drawn, own_key, least, top_value):
    longest = drawn.shape.index(max(drawn.shape))
    spots = []
    for shift in (0, 1):
        where = [jax.random.randint(jax.random.fold_in(own_key, axis), (), 0, length) for axis, length in enumerate(drawn.shape)]
        where[longest] = (where[longest] + shift) % drawn.shape[longest]
        spots.append(tuple(where))
    return drawn.at[spots[0]].set(least).at[spots[1]].set(top_value)


def steps_of(stream_key, extent, shards, least, high):
    gain, own = 1.0, jax.random.fold_in(stream_key, 6)
    for dim, shards_of in shards:
        heights = jnp.exp(jax.random.uniform(jax.random.fold_in(own, dim), (shards_of,), jnp.float32, least / len(shards), high / len(shards)))
        gain = gain * jnp.repeat(heights, extent[dim] // shards_of).reshape([-1 if axis == dim else 1 for axis in range(len(extent))])
    return gain


def gaussian(stream_key, dims, scale, most, cuts=(), held_as=jnp.bfloat16):
    gain = steps_of(stream_key, dims, cuts, -0.22, 0.18) if cuts else 1.0
    array = jax.random.normal(stream_key, dims, jnp.float32) * scale * gain
    return jnp.minimum(jnp.maximum(array, -most), most).astype(held_as)


def setup_inputs(seed: int = 0) -> dict:
    splits = jax.random.split(jax.random.key(seed), 15)
    return {
        "node_feats": gaussian(splits[0], (NODES, WIDTH), 1.0, 6.0, ((0, 128),)),
        "send_block": with_ends(jax.random.randint(splits[1], (PEERS, PEERS, SLOTS), 0, BLOCKS_DEV), jax.random.fold_in(splits[1], 1), 0, BLOCKS_DEV - 1).astype(jnp.int32),
        "recv_block": with_ends(jax.random.randint(splits[2], (PEERS, PEERS, SLOTS), 0, BLOCKS_DEV), jax.random.fold_in(splits[2], 1), 0, BLOCKS_DEV - 1).astype(jnp.int32),
        "recv_rel": with_ends(jax.random.randint(splits[3], (PEERS, PEERS, SLOTS), 0, RELATIONS), jax.random.fold_in(splits[3], 1), 0, RELATIONS - 1).astype(jnp.int32),
        "recv_count": draw_recv_count(jax.random.fold_in(splits[14], 71), 0),
        "recv_adj": draw_recv_adj(jax.random.fold_in(splits[14], 71), 0),
        "local_src": with_ends(jax.random.randint(splits[6], (PEERS, LOCAL_SLOTS), 0, BLOCKS_DEV), jax.random.fold_in(splits[6], 1), 0, BLOCKS_DEV - 1).astype(jnp.int32),
        "local_tgt": with_ends(jax.random.randint(splits[7], (PEERS, LOCAL_SLOTS), 0, BLOCKS_DEV), jax.random.fold_in(splits[7], 1), 0, BLOCKS_DEV - 1).astype(jnp.int32),
        "local_rel": with_ends(jax.random.randint(splits[8], (PEERS, LOCAL_SLOTS), 0, RELATIONS), jax.random.fold_in(splits[8], 1), 0, RELATIONS - 1).astype(jnp.int32),
        "local_adj": draw_local_adj(jax.random.fold_in(splits[14], 71), 0),
        "bases": gaussian(splits[10], (BASES, WIDTH, WIDTH), WIDTH ** -0.5, 0.375),
        "coeffs": gaussian(splits[11], (RELATIONS, BASES), BASES ** -0.5, 2.0),
        "self_weight": gaussian(splits[12], (WIDTH, WIDTH), WIDTH ** -0.5, 0.375),
        "cotangent": gaussian(splits[13], (NODES, WIDTH), 1.0, 6.0, ((0, 128),)),
    }


highest = lax.Precision.HIGHEST

def slot_tables(target_ids, relation_ids, valid_mask, coeffs):
    onehot_tgt = (target_ids[:, None] == jnp.arange(BLOCKS_DEV, dtype=jnp.int32)[None, :]).astype(jnp.float32) * valid_mask[:, None]
    onehot_rel = (relation_ids[:, None] == jnp.arange(RELATIONS, dtype=jnp.int32)[None, :]).astype(jnp.float32)
    coef_rows = jnp.dot(onehot_rel, coeffs.astype(jnp.float32), precision=highest)
    mixing = (onehot_tgt[:, :, None] * coef_rows[:, None, :]).reshape(-1, BLOCKS_DEV * BASES)
    return (onehot_tgt, onehot_rel, mixing)

def reference(node_feats, send_block, recv_block, recv_rel, recv_count, recv_adj, local_src, local_tgt, local_rel, local_adj, bases, coeffs, self_weight, cotangent):
    node_blocks = node_feats.reshape(PEERS, BLOCKS_DEV, BLOCK, WIDTH)
    cot_blocks = cotangent.reshape(PEERS, BLOCKS_DEV, BLOCK, WIDTH)
    senders = jnp.arange(PEERS, dtype=jnp.int32)
    bases_wide = bases.astype(jnp.float32)
    remote = PEERS * SLOTS

    def visit_owner(state_now, owner_id):
        grad_acc, grad_bases, grad_coef = state_now
        chosen = send_block[:, owner_id, :]
        remote_rows = node_blocks[senders[:, None], chosen].reshape(remote, BLOCK, WIDTH)
        local_rows = node_blocks[owner_id][local_src[owner_id]]
        src_rows = jnp.concatenate([remote_rows, local_rows], axis=0)
        adjacency = jnp.concatenate([recv_adj[owner_id].reshape(remote, BLOCK, BLOCK), local_adj[owner_id]], axis=0)
        remote_valid = (jnp.arange(SLOTS, dtype=jnp.int32)[None, :] < recv_count[owner_id][:, None]).astype(jnp.float32).reshape(remote)
        valid_mask = jnp.concatenate([remote_valid, jnp.ones((LOCAL_SLOTS,), jnp.float32)])
        target_ids = jnp.concatenate([recv_block[owner_id].reshape(remote), local_tgt[owner_id]]).astype(jnp.int32)
        relation_ids = jnp.concatenate([recv_rel[owner_id].reshape(remote), local_rel[owner_id]]).astype(jnp.int32)
        onehot_tgt, onehot_rel, mixing = slot_tables(target_ids, relation_ids, valid_mask, coeffs)
        adj_wide = adjacency.astype(jnp.float32)
        aggregated = (jnp.einsum('sij,sjh->sih', adj_wide, src_rows.astype(jnp.float32), precision=highest) * valid_mask[:, None, None]).astype(jnp.bfloat16)
        degree = 1.0 + jnp.dot(onehot_tgt.T, lax.optimization_barrier(jnp.sum(adj_wide, axis=2)), precision=highest)
        row_norm = lax.rsqrt(degree)
        agg_flat = aggregated.reshape(-1, BLOCK * WIDTH).astype(jnp.float32)
        basis_sums = jnp.dot(mixing.T, agg_flat, precision=highest).astype(jnp.bfloat16).reshape(BLOCKS_DEV, BASES, BLOCK, WIDTH)
        sums_wide = basis_sums.astype(jnp.float32)
        mixed_sum = jnp.einsum('tbih,bhk->tik', sums_wide, bases_wide, precision=highest)
        self_term = jnp.einsum('tih,hk->tik', node_blocks[owner_id].astype(jnp.float32), self_weight.astype(jnp.float32), precision=highest)
        out_block = (row_norm[:, :, None] * mixed_sum + self_term).astype(jnp.bfloat16)
        scaled = (row_norm[:, :, None] * cot_blocks[owner_id].astype(jnp.float32)).astype(jnp.bfloat16)
        scaled_wide = scaled.astype(jnp.float32)
        projected = jnp.einsum('tik,bhk->tbih', scaled_wide, bases_wide, precision=highest).astype(jnp.bfloat16)
        proj_flat = projected.reshape(BLOCKS_DEV * BASES, BLOCK * WIDTH).astype(jnp.float32)
        grad_bases = grad_bases + jnp.einsum('tbih,tik->bhk', sums_wide, scaled_wide, precision=highest)
        pair_prods = jnp.dot(agg_flat, proj_flat.T, precision=highest).reshape(-1, BLOCKS_DEV, BASES)
        inner_prod = lax.optimization_barrier(jnp.sum(pair_prods * onehot_tgt[:, :, None], axis=1))
        grad_coef = grad_coef + jnp.dot(onehot_rel.T, inner_prod, precision=highest)
        slot_cot = jnp.dot(mixing, proj_flat, precision=highest).astype(jnp.bfloat16).reshape(-1, BLOCK, WIDTH)
        slot_grad = (jnp.einsum('sij,sih->sjh', adj_wide, slot_cot.astype(jnp.float32), precision=highest) * valid_mask[:, None, None]).astype(jnp.bfloat16).astype(jnp.float32)
        grad_acc = grad_acc.at[senders[:, None], chosen].add(slot_grad[:remote].reshape(PEERS, SLOTS, BLOCK, WIDTH))
        grad_acc = grad_acc.at[owner_id, local_src[owner_id]].add(slot_grad[remote:])
        return ((grad_acc, grad_bases, grad_coef), out_block)
    zero_state = (jnp.zeros((PEERS, BLOCKS_DEV, BLOCK, WIDTH), jnp.float32), jnp.zeros((BASES, WIDTH, WIDTH), jnp.float32), jnp.zeros((RELATIONS, BASES), jnp.float32))
    final_state, out_blocks = lax.scan(visit_owner, zero_state, jnp.arange(PEERS, dtype=jnp.int32))
    grad_acc, grad_bases, grad_coef = final_state
    features_out = out_blocks.reshape(NODES, WIDTH)
    self_back = jnp.dot(cotangent.astype(jnp.float32), self_weight.astype(jnp.float32).T, precision=highest)
    grad_features = (grad_acc.reshape(NODES, WIDTH) + self_back).astype(jnp.bfloat16)
    grad_self = jnp.dot(node_feats.astype(jnp.float32).T, cotangent.astype(jnp.float32), precision=highest)
    grad_scale = 1.0 / math.sqrt(NODES)
    return (features_out, grad_features, grad_bases * grad_scale, grad_coef * grad_scale, grad_self * grad_scale)
```

```python
import functools
import math

import jax
import jax.numpy as jnp
from jax import lax
from jax.experimental import pallas as pl
from jax.experimental.pallas import tpu as pltpu
from jax.sharding import PartitionSpec as P

MESH = pl.DeviceIdType.MESH
MIB = 1 << 20
F32 = jnp.float32
BF16 = jnp.bfloat16
SIDE = 4
CORES = 2
BLOCKS = 8
ROWS = 128
WIDTH = 256
STEP = 8
PARTS = (("x", "y", "z", 0, 48), ("y", "z", "x", 48, 48), ("z", "x", "y", 96, 32))
AXES = ("y", "z", "x")
HOPS = (1, 3, 2)
ANY = pl.BlockSpec(memory_space=pl.ANY)
VMEM = pl.BlockSpec(memory_space=pltpu.VMEM)
SMEM = pl.BlockSpec(memory_space=pltpu.SMEM)


def place():
    src, tgt = lax.axis_index("src"), lax.axis_index("tgt")
    return {"y": src // CORES, "c": src % CORES, "z": tgt // SIDE, "x": tgt % SIDE}


def device(at):
    return (at["y"] * CORES + at["c"], at["z"] * SIDE + at["x"])


def band(at):
    return (at["y"] * CORES + at["c"]) * SIDE * SIDE + at["z"] * SIDE + at["x"]


def moved(me, axis, hop):
    return {**me, axis: (me[axis] + hop) % SIDE}


def line_peers(me, axis):
    peers = []
    for hop in HOPS:
        for flip in (0, 1):
            peers.append((hop, flip, {**moved(me, axis, hop), "c": (me["c"] + flip) % CORES}))
    peers.append((0, 1, {**me, "c": (me["c"] + 1) % CORES}))
    return peers


def greet(peers):
    barrier = pltpu.get_barrier_semaphore()
    for peer in peers:
        pl.semaphore_signal(barrier, inc=1, device_id=device(peer), device_id_type=MESH)
    pl.semaphore_wait(barrier, len(peers))


def plane_dims(last):
    return tuple(a for a in AXES if a != last)


def plane_at(ref, last, **where):
    return ref.at[tuple(where.get(a, slice(None)) for a in plane_dims(last))]


def band_at(ref, last, value, core, row, rows):
    where = {"y": slice(None), "z": slice(None), "x": slice(None), last: value}
    return ref.at[where["y"], core, where["z"], where["x"], :, pl.ds(row, rows), :]


def remote(src, dst, send, recv, peer):
    return pltpu.make_async_remote_copy(
        src_ref=src, dst_ref=dst, send_sem=send, recv_sem=recv, device_id=device(peer), device_id_type=MESH
    )


def gather_kernel(feats, picks, g0, g1, g2, i0, i1, i2, own_sem, s1, r1, s2, r2):
    me = place()
    gathered, ids = (g0, g1, g2), (i0, i1, i2)
    greet([moved(me, axis, hop) for axis in AXES for hop in HOPS])
    first, rest, own = {}, [], []
    for j, (a1, a2, last, row, rows) in enumerate(PARTS):
        for u, (src, dst) in enumerate(
            ((feats.at[:, pl.ds(row, rows), :], gathered[j]), (picks, ids[j]))
        ):
            spot = plane_at(dst, last, **{a1: me[a1], a2: me[a2]})
            copy = pltpu.make_async_copy(src, spot, own_sem.at[j, u])
            copy.start()
            own.append(copy)
    for hop in HOPS:
        for j, (a1, a2, last, row, rows) in enumerate(PARTS):
            for u, (src, dst) in enumerate(
                ((feats.at[:, pl.ds(row, rows), :], gathered[j]), (picks, ids[j]))
            ):
                spot = plane_at(dst, last, **{a1: me[a1], a2: me[a2]})
                copy = remote(src, spot, s1.at[j, u, hop - 1], r1.at[j, u, hop - 1], moved(me, a1, hop))
                copy.start()
                first[j, u, hop] = copy
                copy = remote(src, spot, s2.at[j, u, 0, hop - 1], r2.at[j, u, 0, hop - 1], moved(me, a2, hop))
                copy.start()
                rest.append(copy)
    for back in HOPS:
        for j, (a1, a2, last, row, rows) in enumerate(PARTS):
            for u, dst in enumerate((gathered[j], ids[j])):
                first[j, u, back].wait_recv()
                spot = plane_at(dst, last, **{a1: (me[a1] + SIDE - back) % SIDE, a2: me[a2]})
                for hop in HOPS:
                    copy = remote(
                        spot, spot, s2.at[j, u, back, hop - 1], r2.at[j, u, back, hop - 1], moved(me, a2, hop)
                    )
                    copy.start()
                    rest.append(copy)
    for copy in own:
        copy.wait()
    for copy in first.values():
        copy.wait_send()
    for copy in rest:
        copy.wait()


def gather_plane(feats, picks):
    shapes = [jax.ShapeDtypeStruct((SIDE, SIDE, BLOCKS, rows, WIDTH), BF16) for *_, rows in PARTS]
    shapes += [jax.ShapeDtypeStruct((SIDE, SIDE) + picks.shape, jnp.int32)] * 3
    dma = pltpu.SemaphoreType.DMA
    return pl.pallas_call(
        gather_kernel,
        out_shape=shapes,
        in_specs=[ANY] * 2,
        out_specs=[ANY] * 6,
        scratch_shapes=[dma((3, 2)), dma((3, 2, 3)), dma((3, 2, 3)), dma((3, 2, 4, 3)), dma((3, 2, 4, 3))],
        compiler_params=pltpu.CompilerParams(collective_id=0, has_side_effects=True),
        name="gather_plane",
    )(feats, picks)


def exchange_kernel(g0, g1, g2, i0, i1, i2, incoming, b0, b1, b2, send, recv, own_sem):
    me = place()
    gathered, ids, packed = (g0, g1, g2), (i0, i1, i2), (b0, b1, b2)
    greet([p for axis in AXES for hop, flip, p in line_peers(me, axis) if hop] + [{**me, "c": (me["c"] + 1) % CORES}])
    copies = []

    def pack(j, slot, owner):
        def one(n, _):
            a, b = n // SIDE, n % SIDE
            for c in range(2):
                packed[j][slot, a, b, c] = gathered[j][a, b, ids[j][a, b, c, owner]]
            return 0

        lax.fori_loop(0, SIDE * SIDE, one, 0)

    for n in range(7):
        for j, (a1, a2, last, row, rows) in enumerate(PARTS):
            hop, flip, peer = line_peers(me, last)[n]
            pack(j, n, band(peer))
            copy = remote(
                packed[j].at[n],
                band_at(incoming, last, me[last], me["c"], row, rows),
                send.at[j, n],
                recv.at[j, n],
                peer,
            )
            copy.start()
            copies.append(copy)
    for j, (a1, a2, last, row, rows) in enumerate(PARTS):
        pack(j, 7, band(me))
        copy = pltpu.make_async_copy(
            packed[j].at[7], band_at(incoming, last, me[last], me["c"], row, rows), own_sem.at[j]
        )
        copy.start()
        copies.append(copy)
    for copy in copies:
        copy.wait()


def exchange_picks(gathered, ids):
    dma = pltpu.SemaphoreType.DMA
    return pl.pallas_call(
        exchange_kernel,
        out_shape=jax.ShapeDtypeStruct((SIDE, CORES, SIDE, SIDE, 2, ROWS, WIDTH), BF16),
        in_specs=[VMEM] * 3 + [SMEM] * 3,
        out_specs=ANY,
        scratch_shapes=[pltpu.VMEM((8, SIDE, SIDE, 2, rows, WIDTH), BF16) for *_, rows in PARTS]
        + [dma((3, 7)), dma((3, 7)), dma((3,))],
        compiler_params=pltpu.CompilerParams(collective_id=1, has_side_effects=True, vmem_limit_bytes=48 * MIB),
        name="exchange_picks",
    )(*gathered, *ids)


def return_kernel(grads, r0, r1, r2, send, recv, own_sem):
    me = place()
    returned = (r0, r1, r2)
    greet([p for axis in AXES for hop, flip, p in line_peers(me, axis) if hop] + [{**me, "c": (me["c"] + 1) % CORES}])
    copies = []
    for n in range(7):
        for j, (a1, a2, last, row, rows) in enumerate(PARTS):
            hop, flip, peer = line_peers(me, last)[n]
            copy = remote(
                band_at(grads, last, peer[last], peer["c"], row, rows),
                returned[j].at[me["c"], me[last]],
                send.at[j, n],
                recv.at[j, n],
                peer,
            )
            copy.start()
            copies.append(copy)
    for j, (a1, a2, last, row, rows) in enumerate(PARTS):
        copy = pltpu.make_async_copy(
            band_at(grads, last, me[last], me["c"], row, rows), returned[j].at[me["c"], me[last]], own_sem.at[j]
        )
        copy.start()
        copies.append(copy)
    for copy in copies:
        copy.wait()


def return_grads(grads):
    dma = pltpu.SemaphoreType.DMA
    return pl.pallas_call(
        return_kernel,
        out_shape=[
            jax.ShapeDtypeStruct((CORES, SIDE, SIDE, SIDE, 2, rows, WIDTH), BF16) for *_, rows in PARTS
        ],
        in_specs=[ANY],
        out_specs=[ANY] * 3,
        scratch_shapes=[dma((3, 7)), dma((3, 7)), dma((3,))],
        compiler_params=pltpu.CompilerParams(collective_id=2, has_side_effects=True),
        name="return_grads",
    )(grads)


def scatter_kernel(owners, i0, i1, i2, r0, r1, r2, p0, p1, p2, t0, t1, t2):
    ids, returned, sums, totals = (i0, i1, i2), (r0, r1, r2), (p0, p1, p2), (t0, t1, t2)
    a, b = pl.program_id(0), pl.program_id(1)
    for j in range(3):
        totals[j][...] = jnp.zeros_like(totals[j])
        for n in range(CORES * SIDE):
            for c in range(2):
                block = ids[j][a, b, c, owners[j, n]]
                totals[j][block] += returned[j][n // SIDE, n % SIDE, 0, 0, c].astype(F32)
        sums[j][0, 0] = totals[j][...].astype(BF16)


def scatter_blocks(owners, ids, returned):
    return pl.pallas_call(
        scatter_kernel,
        grid=(SIDE, SIDE),
        out_shape=[jax.ShapeDtypeStruct((SIDE, SIDE, BLOCKS, rows, WIDTH), BF16) for *_, rows in PARTS],
        in_specs=[SMEM] * 4
        + [
            pl.BlockSpec((CORES, SIDE, 1, 1, 2, rows, WIDTH), lambda a, b: (0, 0, a, b, 0, 0, 0))
            for *_, rows in PARTS
        ],
        out_specs=[pl.BlockSpec((1, 1, BLOCKS, rows, WIDTH), lambda a, b: (a, b, 0, 0, 0)) for *_, rows in PARTS],
        scratch_shapes=[pltpu.VMEM((BLOCKS, rows, WIDTH), F32) for *_, rows in PARTS],
        compiler_params=pltpu.CompilerParams(vmem_limit_bytes=32 * MIB),
        name="scatter_blocks",
    )(owners, *ids, *returned)


def reduce_kernel(p0, p1, p2, extra, out, a0, a1_, a2_, q0, q1, q2, b0, b1, b2, s1, r1, s2, r2):
    me = place()
    sums, landed, held, final = (p0, p1, p2), (a0, a1_, a2_), (q0, q1, q2), (b0, b1, b2)
    greet([moved(me, axis, hop) for axis in AXES for hop in HOPS])
    first, second = {}, {}

    def pick(j, near, far):
        a1, a2, last, row, rows = PARTS[j]
        return {a1: near, a2: far}

    for hop in HOPS:
        for j, (a1, a2, last, row, rows) in enumerate(PARTS):
            for k in range(SIDE):
                copy = remote(
                    plane_at(sums[j], last, **{a1: k, a2: (me[a2] + hop) % SIDE}),
                    landed[j].at[hop - 1, k],
                    s1.at[j, hop - 1, k],
                    r1.at[j, hop - 1, k],
                    moved(me, a2, hop),
                )
                copy.start()
                first[j, hop, k] = copy
    for j in range(3):
        for hop in HOPS:
            for k in range(SIDE):
                first[j, hop, k].wait()
    for hop in HOPS + (0,):
        for j, (a1, a2, last, row, rows) in enumerate(PARTS):
            k = (me[a1] + hop) % SIDE
            mine = plane_at(sums[j], last, **{a1: k, a2: me[a2]})

            def add(n, _, j=j, k=k, hop=hop, mine=mine):
                total = mine[n].astype(F32)
                for h in range(3):
                    total = total + landed[j][h, k, n].astype(F32)
                held[j][hop, n] = total.astype(BF16)
                return 0

            lax.fori_loop(0, BLOCKS, add, 0)
            if hop:
                copy = remote(
                    held[j].at[hop],
                    final[j].at[hop - 1],
                    s2.at[j, hop - 1],
                    r2.at[j, hop - 1],
                    moved(me, a1, hop),
                )
                copy.start()
                second[j, hop] = copy
    for copy in second.values():
        copy.wait()
    for j, (a1, a2, last, row, rows) in enumerate(PARTS):

        def end(n, _, j=j, row=row, rows=rows):
            total = extra[n, pl.ds(row, rows), :] + held[j][0, n].astype(F32)
            for h in range(3):
                total = total + final[j][h, n].astype(F32)
            out[n, pl.ds(row, rows), :] = total.astype(BF16)
            return 0

        lax.fori_loop(0, BLOCKS, end, 0)


def reduce_plane(sums, extra):
    dma = pltpu.SemaphoreType.DMA
    return pl.pallas_call(
        reduce_kernel,
        out_shape=jax.ShapeDtypeStruct((BLOCKS, ROWS, WIDTH), BF16),
        in_specs=[VMEM] * 4,
        out_specs=VMEM,
        scratch_shapes=[pltpu.VMEM((3, SIDE, BLOCKS, rows, WIDTH), BF16) for *_, rows in PARTS]
        + [pltpu.VMEM((SIDE, BLOCKS, rows, WIDTH), BF16) for *_, rows in PARTS]
        + [pltpu.VMEM((3, BLOCKS, rows, WIDTH), BF16) for *_, rows in PARTS]
        + [dma((3, 3, SIDE)), dma((3, 3, SIDE)), dma((3, 3)), dma((3, 3))],
        compiler_params=pltpu.CompilerParams(collective_id=3, has_side_effects=True, vmem_limit_bytes=48 * MIB),
        name="reduce_plane",
    )(*sums, extra)


def slot_specs(remote_steps):
    return [
        pl.BlockSpec((STEP, ROWS, ROWS), lambda i: (jnp.minimum(i, remote_steps - 1), 0, 0)),
        pl.BlockSpec((STEP, ROWS, ROWS), lambda i: (jnp.maximum(i - remote_steps, 0), 0, 0)),
    ]


def whole(shape):
    return pl.BlockSpec(shape, lambda i: (0,) * len(shape), pipeline_mode=pl.Buffered(1))


def degree_kernel(remote_steps, tgt, valid, remote_adj, local_adj, cot, scaled, norm, total):
    i = pl.program_id(0)

    @pl.when(i == 0)
    def _():
        total[...] = jnp.zeros_like(total)

    def add(adj):
        for l in range(STEP):
            s = i * STEP + l
            total[tgt[s]] += adj[l].astype(F32) * valid[s]

    @pl.when(i < remote_steps)
    def _():
        add(remote_adj)

    @pl.when(i >= remote_steps)
    def _():
        add(local_adj)

    @pl.when(i == pl.num_programs(0) - 1)
    def _():
        for t in range(BLOCKS):
            row_norm = lax.rsqrt(1.0 + jnp.sum(total[t], axis=1, keepdims=True))
            scaled[t] = (cot[t].astype(F32) * row_norm).astype(BF16)
            norm[t] = jnp.broadcast_to(row_norm, (ROWS, ROWS))


def degrees(tgt, valid, remote_adj, local_adj, cot):
    remote_steps, local_steps = remote_adj.shape[0] // STEP, local_adj.shape[0] // STEP
    return pl.pallas_call(
        functools.partial(degree_kernel, remote_steps),
        grid=(remote_steps + local_steps,),
        out_shape=[
            jax.ShapeDtypeStruct((BLOCKS, ROWS, WIDTH), BF16),
            jax.ShapeDtypeStruct((BLOCKS, ROWS, ROWS), F32),
        ],
        in_specs=[SMEM] * 2 + slot_specs(remote_steps) + [whole((BLOCKS, ROWS, WIDTH))],
        out_specs=[whole((BLOCKS, ROWS, WIDTH)), whole((BLOCKS, ROWS, ROWS))],
        scratch_shapes=[pltpu.VMEM((BLOCKS, ROWS, ROWS), F32)],
        compiler_params=pltpu.CompilerParams(vmem_limit_bytes=32 * MIB),
        name="degrees",
    )(tgt, valid, remote_adj, local_adj, cot)


def weight_kernel(coeffs, bases, scaled, weights, cots):
    r = pl.program_id(0)
    for n in range(8):
        rows = pl.ds(n * 32, 32)
        total = coeffs[r, 0] * bases[0, rows, :].astype(F32)
        for b in range(1, 8):
            total = total + coeffs[r, b] * bases[b, rows, :].astype(F32)
        weights[0, rows, :] = total.astype(BF16)
    cots[0] = lax.dot_general(
        scaled[...], weights[0], (((1,), (1,)), ((), ())), preferred_element_type=F32
    ).astype(BF16)


def mix_weights(coeffs, bases, scaled):
    relations = coeffs.shape[0]
    nodes = BLOCKS * ROWS
    return pl.pallas_call(
        weight_kernel,
        grid=(relations,),
        out_shape=[
            jax.ShapeDtypeStruct((relations, WIDTH, WIDTH), BF16),
            jax.ShapeDtypeStruct((relations, nodes, WIDTH), BF16),
        ],
        in_specs=[SMEM, whole(bases.shape), whole((nodes, WIDTH))],
        out_specs=[
            pl.BlockSpec((1, WIDTH, WIDTH), lambda r: (r, 0, 0)),
            pl.BlockSpec((1, nodes, WIDTH), lambda r: (r, 0, 0)),
        ],
        compiler_params=pltpu.CompilerParams(vmem_limit_bytes=32 * MIB),
        name="mix_weights",
    )(coeffs, bases, scaled)


def backward_kernel(remote_steps, tgt, rel, valid, src, remote_adj, local_adj, cots, cot, self_weight, grads, extra):
    i = pl.program_id(0)

    @pl.when(i == 0)
    def _():
        for t in range(BLOCKS):
            extra[t] = lax.dot_general(
                cot[t], self_weight[...], (((1,), (1,)), ((), ())), preferred_element_type=F32
            )

    def grad(adj, l):
        s = i * STEP + l
        return lax.dot_general(
            adj[l], cots[rel[s], tgt[s]], (((0,), (0,)), ((), ())), preferred_element_type=F32
        )

    @pl.when(i < remote_steps)
    def _():
        for l in range(STEP):
            grads[l] = (grad(remote_adj, l) * valid[i * STEP + l]).astype(BF16)

    @pl.when(i >= remote_steps)
    def _():
        for l in range(STEP):
            extra[src[(i - remote_steps) * STEP + l]] += grad(local_adj, l).astype(BF16).astype(F32)


def backward_slots(tgt, rel, valid, src, remote_adj, local_adj, cots, cot, self_weight):
    remote_steps, local_steps = remote_adj.shape[0] // STEP, local_adj.shape[0] // STEP
    return pl.pallas_call(
        functools.partial(backward_kernel, remote_steps),
        grid=(remote_steps + local_steps,),
        out_shape=[
            jax.ShapeDtypeStruct((remote_adj.shape[0], ROWS, WIDTH), BF16),
            jax.ShapeDtypeStruct((BLOCKS, ROWS, WIDTH), F32),
        ],
        in_specs=[SMEM] * 4
        + slot_specs(remote_steps)
        + [whole(cots.shape), whole((BLOCKS, ROWS, WIDTH)), whole((WIDTH, WIDTH))],
        out_specs=[
            pl.BlockSpec((STEP, ROWS, WIDTH), lambda i: (jnp.minimum(i, remote_steps - 1), 0, 0)),
            whole((BLOCKS, ROWS, WIDTH)),
        ],
        compiler_params=pltpu.CompilerParams(vmem_limit_bytes=48 * MIB),
        name="backward_slots",
    )(tgt, rel, valid, src, remote_adj, local_adj, cots, cot, self_weight)


def forward_kernel(
    remote_steps, tgt, rel, valid, src, coeffs, remote_adj, local_adj, incoming, feats, weights, scaled, cot, norm,
    self_weight, bases, out, terms, mixed, outer,
):
    i = pl.program_id(0)

    @pl.when(i == 0)
    def _():
        mixed[...] = jnp.zeros_like(mixed)
        outer[...] = jnp.zeros_like(outer)

    def visit(adj, rows, s):
        aggregated = (jnp.dot(adj, rows, preferred_element_type=F32) * valid[s]).astype(BF16)
        mixed[tgt[s]] += jnp.dot(aggregated, weights[rel[s]], preferred_element_type=F32)
        outer[rel[s]] += lax.dot_general(
            aggregated, scaled[tgt[s]], (((0,), (0,)), ((), ())), preferred_element_type=F32
        )

    @pl.when(i < remote_steps)
    def _():
        for l in range(STEP):
            visit(remote_adj[l], incoming[l], i * STEP + l)

    @pl.when(i >= remote_steps)
    def _():
        for l in range(STEP):
            visit(local_adj[l], feats[src[(i - remote_steps) * STEP + l]], i * STEP + l)

    @pl.when(i == pl.num_programs(0) - 1)
    def _():
        relations = outer.shape[0]
        basis_count = bases.shape[0]
        for t in range(BLOCKS):
            own = jnp.dot(feats[t], self_weight[...], preferred_element_type=F32)
            for half in range(2):
                cols = pl.ds(half * ROWS, ROWS)
                out[t, :, cols] = (
                    norm[t] * mixed[t, :, cols] + own[:, half * ROWS : (half + 1) * ROWS]
                ).astype(BF16)
        self_grad = jnp.zeros((WIDTH, WIDTH), F32)
        for t in range(BLOCKS):
            self_grad += lax.dot_general(feats[t], cot[t], (((0,), (0,)), ((), ())), preferred_element_type=F32)
        terms[pl.ds(basis_count * WIDTH, WIDTH), :] = self_grad

        def mix(n, _):
            rows = pl.ds(n * 8, 8)
            totals = [jnp.zeros((8, WIDTH), F32) for _ in range(basis_count)]
            for r in range(relations):
                piece = outer[r, rows, :]
                totals = [totals[b] + coeffs[r, b] * piece for b in range(basis_count)]
            for b in range(basis_count):
                terms[pl.ds(b * WIDTH + n * 8, 8), :] = totals[b]
            return 0

        lax.fori_loop(0, WIDTH // 8, mix, 0)

        def inner(r, _):
            def part(n, totals):
                rows = pl.ds(n * 16, 16)
                piece = outer[r, rows, :]
                return tuple(totals[b] + piece * bases[b, rows, :].astype(F32) for b in range(basis_count))

            totals = lax.fori_loop(
                0, WIDTH // 16, part, tuple(jnp.zeros((16, WIDTH), F32) for _ in range(basis_count))
            )
            rows = [jnp.sum(total, axis=0, keepdims=True) for total in totals]
            terms[pl.ds((basis_count + 1) * WIDTH + r * basis_count, basis_count), :] = jnp.concatenate(rows, axis=0)
            return 0

        lax.fori_loop(0, relations, inner, 0)


def forward_slots(
    tgt, rel, valid, src, coeffs, remote_adj, local_adj, incoming, feats, weights, scaled, cot, norm, self_weight, bases
):
    remote_steps, local_steps = remote_adj.shape[0] // STEP, local_adj.shape[0] // STEP
    relations, basis_count = coeffs.shape
    term_rows = (basis_count + 1) * WIDTH + relations * basis_count
    return pl.pallas_call(
        functools.partial(forward_kernel, remote_steps),
        grid=(remote_steps + local_steps,),
        out_shape=[
            jax.ShapeDtypeStruct((BLOCKS, ROWS, WIDTH), BF16),
            jax.ShapeDtypeStruct((term_rows, WIDTH), F32),
        ],
        in_specs=[SMEM] * 5
        + slot_specs(remote_steps)
        + [pl.BlockSpec((STEP, ROWS, WIDTH), lambda i: (jnp.minimum(i, remote_steps - 1), 0, 0))]
        + [whole(a.shape) for a in (feats, weights, scaled, cot, norm, self_weight, bases)],
        out_specs=[whole((BLOCKS, ROWS, WIDTH)), whole((term_rows, WIDTH))],
        scratch_shapes=[
            pltpu.VMEM((BLOCKS, ROWS, WIDTH), F32),
            pltpu.VMEM((relations, WIDTH, WIDTH), F32),
        ],
        compiler_params=pltpu.CompilerParams(vmem_limit_bytes=48 * MIB),
        name="forward_slots",
    )(tgt, rel, valid, src, coeffs, remote_adj, local_adj, incoming, feats, weights, scaled, cot, norm, self_weight, bases)


def local(
    node_feats, send_block, recv_block, recv_rel, recv_count, recv_adj, local_src, local_tgt, local_rel, local_adj,
    bases, coeffs, self_weight, cotangent,
):
    peers = lax.axis_size(("src", "tgt"))
    slot_cap = send_block.shape[2]
    remote_slots = peers * slot_cap
    relations, basis_count = coeffs.shape
    feats = node_feats.reshape(BLOCKS, ROWS, WIDTH)
    cot = cotangent.reshape(BLOCKS, ROWS, WIDTH)
    me = place()
    gathered_ids = gather_plane(feats, send_block[0].T)
    gathered, ids = gathered_ids[:3], gathered_ids[3:]
    incoming = exchange_picks(gathered, ids).reshape(remote_slots, ROWS, WIDTH)

    remote_adj = recv_adj.reshape(remote_slots, ROWS, ROWS)
    own_adj = local_adj[0]
    src = local_src[0]
    tgt = jnp.concatenate([recv_block.reshape(remote_slots), local_tgt[0]])
    rel = jnp.concatenate([recv_rel.reshape(remote_slots), local_rel[0]])
    remote_valid = (jnp.arange(slot_cap, dtype=jnp.int32)[None, :] < recv_count[0][:, None]).astype(F32)
    valid = jnp.concatenate([remote_valid.reshape(remote_slots), jnp.ones((src.shape[0],), F32)])
    wide_coeffs = coeffs.astype(F32)
    scaled, norm = degrees(tgt, valid, remote_adj, own_adj, cot)
    weights, cots = mix_weights(wide_coeffs, bases, scaled.reshape(BLOCKS * ROWS, WIDTH))
    cots = cots.reshape(relations, BLOCKS, ROWS, WIDTH)
    grads, extra = backward_slots(tgt, rel, valid, src, remote_adj, own_adj, cots, cot, self_weight)
    features_out, terms = forward_slots(
        tgt, rel, valid, src, wide_coeffs, remote_adj, own_adj, incoming, feats, weights, scaled, cot, norm,
        self_weight, bases,
    )
    totals = lax.psum(terms, ("src", "tgt"))
    returned = return_grads(grads.reshape(SIDE, CORES, SIDE, SIDE, slot_cap, ROWS, WIDTH))
    owners = jnp.stack(
        [
            jnp.stack([band({**me, "c": core, last: k}) for core in range(CORES) for k in range(SIDE)])
            for _, _, last, _, _ in PARTS
        ]
    ).astype(jnp.int32)
    sums = scatter_blocks(owners, ids, returned)
    grad_features = reduce_plane(sums, extra)
    totals = totals * (1.0 / math.sqrt(node_feats.shape[0] * peers))
    basis_rows = basis_count * WIDTH
    return (
        features_out.reshape(node_feats.shape),
        grad_features.reshape(node_feats.shape),
        totals[:basis_rows].reshape(basis_count, WIDTH, WIDTH),
        jnp.sum(totals[basis_rows + WIDTH :], axis=1).reshape(relations, basis_count),
        totals[basis_rows : basis_rows + WIDTH],
    )


def solution(mesh):
    both = ("src", "tgt")
    in_specs = (
        P(both, None),
        P(both, None, None),
        P(both, None, None),
        P(both, None, None),
        P(both, None),
        P(both, None, None, None, None),
        P(both, None),
        P(both, None),
        P(both, None),
        P(both, None, None, None),
        P(),
        P(),
        P(),
        P(both, None),
    )
    out_specs = (P(both, None), P(both, None), P(), P(), P())
    return jax.shard_map(local, mesh=mesh, in_specs=in_specs, out_specs=out_specs, check_vma=False)
```

```python
import functools
import math

import jax
import jax.numpy as jnp
from jax import lax
from jax.experimental import pallas as pl
from jax.experimental.pallas import tpu as pltpu
from jax.sharding import PartitionSpec as P

MESH = pl.DeviceIdType.MESH
MIB = 1 << 20
F32 = jnp.float32
BF16 = jnp.bfloat16
SIDE = 4
CORES = 2
BLOCKS = 8
ROWS = 128
WIDTH = 256
STEP = 8
WIDE = 32
CHUNKS = 8
TERM_ROWS = 8
TERMS = CORES * 3 * SIDE**3 * TERM_ROWS
PARTS = (("x", "y", "z", 0, 48), ("y", "z", "x", 48, 48), ("z", "x", "y", 96, 32))
AXES = ("y", "z", "x")
HOPS = (1, 3, 2)
ANY = pl.BlockSpec(memory_space=pl.ANY)
VMEM = pl.BlockSpec(memory_space=pltpu.VMEM)
SMEM = pl.BlockSpec(memory_space=pltpu.SMEM)


def place():
    src, tgt = lax.axis_index("src"), lax.axis_index("tgt")
    return {"y": src // CORES, "c": src % CORES, "z": tgt // SIDE, "x": tgt % SIDE}


def device(at):
    return (at["y"] * CORES + at["c"], at["z"] * SIDE + at["x"])


def band(at):
    return (at["y"] * CORES + at["c"]) * SIDE * SIDE + at["z"] * SIDE + at["x"]


def moved(me, axis, hop):
    return {**me, axis: (me[axis] + hop) % SIDE}


def line_peers(me, axis):
    peers = []
    for hop in HOPS:
        for flip in (0, 1):
            peers.append((hop, flip, {**moved(me, axis, hop), "c": (me["c"] + flip) % CORES}))
    peers.append((0, 1, {**me, "c": (me["c"] + 1) % CORES}))
    return peers


def greet(peers):
    barrier = pltpu.get_barrier_semaphore()
    for peer in peers:
        pl.semaphore_signal(barrier, inc=1, device_id=device(peer), device_id_type=MESH)
    pl.semaphore_wait(barrier, len(peers))


def plane_dims(last):
    return tuple(a for a in AXES if a != last)


def plane_at(ref, last, **where):
    return ref.at[tuple(where.get(a, slice(None)) for a in plane_dims(last))]


def band_at(ref, core, row, rows, **where):
    where = {"y": slice(None), "z": slice(None), "x": slice(None), **where}
    return ref.at[where["y"], core, where["z"], where["x"], :, pl.ds(row, rows), :]


def remote(src, dst, send, recv, peer):
    return pltpu.make_async_remote_copy(
        src_ref=src, dst_ref=dst, send_sem=send, recv_sem=recv, device_id=device(peer), device_id_type=MESH
    )


def gather_kernel(
    coeffs, tgt, rel, valid, src, feats, picks, bases, scaled, cot, self_weight, remote_adj, local_adj,
    g0, g1, g2, i0, i1, i2, weights, extra, grads,
    adj, own_adj, cots, staged, part, own_sem, s1, r1, s2, r2, adj_sem, out_sem,
):
    me = place()
    gathered, ids = (g0, g1, g2), (i0, i1, i2)
    relations, remote_slots, local_slots = cots.shape[0], adj.shape[0], own_adj.shape[0]
    chunk = remote_slots // CHUNKS
    adj_copies = [
        pltpu.make_async_copy(remote_adj, adj, adj_sem.at[0]),
        pltpu.make_async_copy(local_adj, own_adj, adj_sem.at[1]),
    ]
    for copy in adj_copies:
        copy.start()
    greet([moved(me, axis, hop) for axis in AXES for hop in HOPS])
    first, rest, own = {}, [], []
    jobs = [
        (j, u, a1, a2, last, from_, to)
        for j, (a1, a2, last, row, rows) in enumerate(PARTS)
        for u, (from_, to) in enumerate(((feats.at[:, pl.ds(row, rows), :], gathered[j]), (picks, ids[j])))
    ]
    for hop in HOPS:
        for j, u, a1, a2, last, from_, to in jobs:
            spot = plane_at(to, last, **{a1: me[a1], a2: me[a2]})
            copy = remote(from_, spot, s1.at[j, u, hop - 1], r1.at[j, u, hop - 1], moved(me, a1, hop))
            copy.start()
            first[j, u, hop] = copy
    for hop in HOPS:
        for j, u, a1, a2, last, from_, to in jobs:
            spot = plane_at(to, last, **{a1: me[a1], a2: me[a2]})
            copy = remote(from_, spot, s2.at[j, u, 0, hop - 1], r2.at[j, u, 0, hop - 1], moved(me, a2, hop))
            copy.start()
            rest.append(copy)
    for j, u, a1, a2, last, from_, to in jobs:
        spot = plane_at(to, last, **{a1: me[a1], a2: me[a2]})
        copy = pltpu.make_async_copy(from_, spot, own_sem.at[j, u])
        copy.start()
        own.append(copy)

    def mix(r, _):
        for n in range(8):
            rows = pl.ds(n * 32, 32)
            total = coeffs[r, 0] * bases[0, rows, :].astype(F32)
            for b in range(1, 8):
                total = total + coeffs[r, b] * bases[b, rows, :].astype(F32)
            weights[r, rows, :] = total.astype(BF16)
        for t in range(BLOCKS):
            cots[r, t] = lax.dot_general(
                scaled[t], weights[r], (((1,), (1,)), ((), ())), preferred_element_type=F32
            ).astype(BF16)
        return 0

    third = relations // 3
    for n, back in enumerate(HOPS):
        lax.fori_loop(n * third, (n + 1) * third if n < 2 else relations, mix, 0)
        for j, u, a1, a2, last, from_, to in jobs:
            first[j, u, back].wait_recv()
            spot = plane_at(to, last, **{a1: (me[a1] + SIDE - back) % SIDE, a2: me[a2]})
            for hop in HOPS:
                copy = remote(spot, spot, s2.at[j, u, back, hop - 1], r2.at[j, u, back, hop - 1], moved(me, a2, hop))
                copy.start()
                rest.append(copy)

    for copy in adj_copies:
        copy.wait()

    def slot_chunk(k):
        return pltpu.make_async_copy(
            staged.at[pl.ds(k * chunk, chunk)], grads.at[pl.ds(k * chunk, chunk)], out_sem.at[k]
        )

    def remote_chunk(k, _):
        def group(g, _):
            for l in range(STEP):
                s = k * chunk + g * STEP + l
                grad = lax.dot_general(
                    adj[s], cots[rel[s], tgt[s]], (((0,), (0,)), ((), ())), preferred_element_type=F32
                )
                staged[s] = (grad * valid[s]).astype(BF16)
            return 0

        lax.fori_loop(0, chunk // STEP, group, 0)
        slot_chunk(k).start()
        return 0

    lax.fori_loop(0, CHUNKS, remote_chunk, 0)
    for t in range(BLOCKS):
        extra[t] = lax.dot_general(cot[t], self_weight[...], (((1,), (1,)), ((), ())), preferred_element_type=F32)

    def local_group(g, _):
        for l in range(STEP):
            s = remote_slots + g * STEP + l
            part[l] = lax.dot_general(
                own_adj[g * STEP + l], cots[rel[s], tgt[s]], (((0,), (0,)), ((), ())), preferred_element_type=F32
            ).astype(BF16)
        for k in range(BLOCKS):
            hits = [(src[g * STEP + l] == k).astype(F32) for l in range(STEP)]
            for n in range(4):
                rows = pl.ds(n * 32, 32)
                total = extra[k, rows, :]
                for l in range(STEP):
                    total = total + hits[l] * part[l, rows, :].astype(F32)
                extra[k, rows, :] = total
        return 0

    lax.fori_loop(0, local_slots // STEP, local_group, 0)

    def end_chunk(k, _):
        slot_chunk(k).wait()
        return 0

    lax.fori_loop(0, CHUNKS, end_chunk, 0)
    for copy in own:
        copy.wait()
    for copy in first.values():
        copy.wait_send()
    for copy in rest:
        copy.wait()


def gather_plane(coeffs, tgt, rel, valid, src, feats, picks, bases, scaled, cot, self_weight, remote_adj, local_adj):
    relations, remote_slots = coeffs.shape[0], remote_adj.shape[0]
    shapes = [jax.ShapeDtypeStruct((SIDE, SIDE, BLOCKS, rows, WIDTH), BF16) for *_, rows in PARTS]
    shapes += [jax.ShapeDtypeStruct((SIDE, SIDE) + picks.shape, jnp.int32)] * 3
    shapes += [
        jax.ShapeDtypeStruct((relations, WIDTH, WIDTH), BF16),
        jax.ShapeDtypeStruct((BLOCKS, ROWS, WIDTH), F32),
        jax.ShapeDtypeStruct((remote_slots, ROWS, WIDTH), BF16),
    ]
    dma = pltpu.SemaphoreType.DMA
    return pl.pallas_call(
        gather_kernel,
        out_shape=shapes,
        in_specs=[SMEM] * 5 + [ANY] * 2 + [VMEM] * 4 + [ANY] * 2,
        out_specs=[ANY] * 6 + [VMEM] * 2 + [ANY],
        scratch_shapes=[
            pltpu.VMEM(remote_adj.shape, BF16),
            pltpu.VMEM(local_adj.shape, BF16),
            pltpu.VMEM((relations, BLOCKS, ROWS, WIDTH), BF16),
            pltpu.VMEM((remote_slots, ROWS, WIDTH), BF16),
            pltpu.VMEM((STEP, ROWS, WIDTH), BF16),
            dma((3, 2)), dma((3, 2, 3)), dma((3, 2, 3)), dma((3, 2, 4, 3)), dma((3, 2, 4, 3)),
            dma((2,)), dma((CHUNKS,)),
        ],
        compiler_params=pltpu.CompilerParams(collective_id=0, has_side_effects=True, vmem_limit_bytes=58 * MIB),
        name="gather_plane",
    )(coeffs, tgt, rel, valid, src, feats, picks, bases, scaled, cot, self_weight, remote_adj, local_adj)


def exchange_kernel(g0, g1, g2, i0, i1, i2, incoming, b0, b1, b2, send, recv, own_sem):
    me = place()
    gathered, ids, packed = (g0, g1, g2), (i0, i1, i2), (b0, b1, b2)
    greet([p for axis in AXES for hop, flip, p in line_peers(me, axis) if hop] + [{**me, "c": (me["c"] + 1) % CORES}])
    copies = []

    def pack(j, slot, owner):
        def one(n, _):
            a, b = n // SIDE, n % SIDE
            for c in range(2):
                packed[j][slot, a, b, c] = gathered[j][a, b, ids[j][a, b, c, owner]]
            return 0

        lax.fori_loop(0, SIDE * SIDE, one, 0)

    for n in range(7):
        for j, (a1, a2, last, row, rows) in enumerate(PARTS):
            hop, flip, peer = line_peers(me, last)[n]
            pack(j, n, band(peer))
            copy = remote(
                packed[j].at[n],
                band_at(incoming, me["c"], row, rows, **{last: me[last]}),
                send.at[j, n],
                recv.at[j, n],
                peer,
            )
            copy.start()
            copies.append(copy)
    for j, (a1, a2, last, row, rows) in enumerate(PARTS):
        pack(j, 7, band(me))
        copy = pltpu.make_async_copy(
            packed[j].at[7], band_at(incoming, me["c"], row, rows, **{last: me[last]}), own_sem.at[j]
        )
        copy.start()
        copies.append(copy)
    for copy in copies:
        copy.wait()


def exchange_picks(gathered, ids):
    dma = pltpu.SemaphoreType.DMA
    return pl.pallas_call(
        exchange_kernel,
        out_shape=jax.ShapeDtypeStruct((SIDE, CORES, SIDE, SIDE, 2, ROWS, WIDTH), BF16),
        in_specs=[VMEM] * 3 + [SMEM] * 3,
        out_specs=ANY,
        scratch_shapes=[pltpu.VMEM((8, SIDE, SIDE, 2, rows, WIDTH), BF16) for *_, rows in PARTS]
        + [dma((3, 7)), dma((3, 7)), dma((3,))],
        compiler_params=pltpu.CompilerParams(collective_id=1, has_side_effects=True, vmem_limit_bytes=48 * MIB),
        name="exchange_picks",
    )(*gathered, *ids)


def return_kernel(
    scale, i0, i1, i2, grads, extra, terms, out, full,
    r0, r1, r2, p0, p1, p2, l0, l1, l2, q0, q1, q2, f0, f1, f2, added, h0, b0, h1, b1, h2, b2, b3,
    send, recv, own_sem, s1, v1, s2, v2, pair_sem, ws, wr,
):
    me = place()
    ids, returned, sums, landed = (i0, i1, i2), (r0, r1, r2), (p0, p1, p2), (l0, l1, l2)
    held, final = (q0, q1, q2), (f0, f1, f2)
    core, partner = me["c"], {**me, "c": (me["c"] + 1) % CORES}
    own = [
        pltpu.make_async_copy(terms.at[core], h0, own_sem.at[3]),
        pltpu.make_async_copy(extra, added, own_sem.at[4]),
    ]
    for j, (a1, a2, last, row, rows) in enumerate(PARTS):
        own.append(
            pltpu.make_async_copy(
                band_at(grads, core, row, rows, **{last: me[last]}), returned[j].at[core, me[last]], own_sem.at[j]
            )
        )
    for copy in own:
        copy.start()
    greet([p for axis in AXES for hop, flip, p in line_peers(me, axis) if hop] + [partner])
    halves = remote(terms.at[partner["c"]], b0, pair_sem.at[0], pair_sem.at[1], partner)
    halves.start()
    sent = [[], [], [], []]

    def give(group):
        for n in range(7):
            for j, (a1, a2, last, row, rows) in enumerate(PARTS):
                hop, flip, peer = line_peers(me, last)[n]
                far = (me[a2] + group) % SIDE
                copy = remote(
                    band_at(grads, peer["c"], row, rows, **{last: peer[last], a2: far}),
                    plane_at(returned[j].at[core, me[last]], last, **{a2: far}),
                    send.at[j, n, group],
                    recv.at[j, n, group],
                    peer,
                )
                copy.start()
                sent[group].append(copy)

    def weigh(stage, level, src, dst):
        copies = []
        for hop in HOPS:
            for j, part in enumerate(PARTS):
                axis = part[level]
                copy = remote(
                    src(j, (me[axis] + hop) % SIDE),
                    dst(j, hop - 1),
                    ws.at[stage, j, hop - 1],
                    wr.at[stage, j, hop - 1],
                    moved(me, axis, hop),
                )
                copy.start()
                copies.append(copy)
        return copies

    def done(copies):
        for copy in copies:
            copy.wait()

    def piece(j, depth):
        spot = (core, j) + tuple(me[PARTS[j][level]] for level in (2, 1, 0)[:depth])
        return full.at[spot]

    def fold(j, hop, k):
        a1, a2, last, row, rows = PARTS[j]
        where = {a1: k, a2: (me[a2] + hop) % SIDE}
        spot = tuple(where[a] for a in plane_dims(last))

        def two(n, _):
            totals = [jnp.zeros((rows, WIDTH), F32)] * 2
            for other in range(CORES):
                for place_on in range(SIDE):
                    owner = band({**me, "c": other, last: place_on})
                    for c in range(2):
                        block = ids[j][spot + (c, owner)]
                        grad = returned[j][(other, place_on) + spot + (c,)].astype(F32)
                        totals = [totals[h] + (block == 2 * n + h).astype(F32) * grad for h in range(2)]
            for h in range(2):
                sums[j][spot + (2 * n + h,)] = totals[h].astype(BF16)
            return 0

        lax.fori_loop(0, BLOCKS // 2, two, 0)

    def across(j, hop, k):
        a1, a2, last, row, rows = PARTS[j]
        return remote(
            plane_at(sums[j], last, **{a1: k, a2: (me[a2] + hop) % SIDE}),
            landed[j].at[hop - 1, k],
            s1.at[j, hop - 1, k],
            v1.at[j, hop - 1, k],
            moved(me, a2, hop),
        )

    def bands(group):
        done(sent[group])

        def one(k, _):
            for j in range(3):
                fold(j, group, k)
                if group:
                    across(j, group, k).start()
            return 0

        lax.fori_loop(0, SIDE, one, 0)

    give(1)
    own[0].wait()
    halves.wait()
    h0[...] = h0[...] + b0[...]
    stage = weigh(0, 2, lambda j, k: h0.at[j, k], lambda j, h: b1.at[j, h])
    give(3)
    for copy in own[1:]:
        copy.wait()
    bands(1)
    done(stage)
    for j, part in enumerate(PARTS):
        h1[j] = h0[j, me[part[2]]] + b1[j, 0] + b1[j, 1] + b1[j, 2]
    stage = weigh(1, 1, lambda j, k: h1.at[j, k], lambda j, h: b2.at[j, h])
    give(2)
    bands(3)
    done(stage)
    for j, part in enumerate(PARTS):
        h2[j] = h1[j, me[part[1]]] + b2[j, 0] + b2[j, 1] + b2[j, 2]
    stage = weigh(2, 0, lambda j, k: h2.at[j, k], lambda j, h: b3.at[j, h])
    give(0)
    bands(2)
    done(stage)
    for j, part in enumerate(PARTS):
        piece(j, 3)[...] = (h2[j, me[part[0]]] + b3[j, 0] + b3[j, 1] + b3[j, 2]) * scale[0]
    stage = weigh(3, 0, lambda j, k: piece(j, 3), lambda j, h: piece(j, 3))
    bands(0)
    done(stage)
    stage = weigh(4, 1, lambda j, k: piece(j, 2), lambda j, h: piece(j, 2))
    for hop in HOPS:
        for j in range(3):
            for k in range(SIDE):
                across(j, hop, k).wait()
    done(stage)
    stage = weigh(5, 2, lambda j, k: piece(j, 1), lambda j, h: piece(j, 1))
    second = []
    for hop in HOPS + (0,):
        for j, (a1, a2, last, row, rows) in enumerate(PARTS):
            k = (me[a1] + hop) % SIDE
            mine = plane_at(sums[j], last, **{a1: k, a2: me[a2]})

            def add(n, _, j=j, k=k, hop=hop, mine=mine):
                total = mine[n].astype(F32)
                for h in range(3):
                    total = total + landed[j][h, k, n].astype(F32)
                held[j][hop, n] = total.astype(BF16)
                return 0

            lax.fori_loop(0, BLOCKS, add, 0)
            if hop:
                copy = remote(
                    held[j].at[hop], final[j].at[hop - 1], s2.at[j, hop - 1], v2.at[j, hop - 1], moved(me, a1, hop)
                )
                copy.start()
                second.append(copy)
    done(stage)
    back = remote(full.at[core], full.at[core], pair_sem.at[2], pair_sem.at[3], partner)
    back.start()
    done(second)
    for j, (a1, a2, last, row, rows) in enumerate(PARTS):

        def end(n, _, j=j, row=row, rows=rows):
            total = added[n, pl.ds(row, rows), :] + held[j][0, n].astype(F32)
            for h in range(3):
                total = total + final[j][h, n].astype(F32)
            out[n, pl.ds(row, rows), :] = total.astype(BF16)
            return 0

        lax.fori_loop(0, BLOCKS, end, 0)
    back.wait()


def return_grads(scale, ids, grads, extra, terms):
    dma = pltpu.SemaphoreType.DMA
    piece = (TERM_ROWS, WIDTH)
    return pl.pallas_call(
        return_kernel,
        out_shape=[
            jax.ShapeDtypeStruct((BLOCKS, ROWS, WIDTH), BF16),
            jax.ShapeDtypeStruct((CORES, 3, SIDE, SIDE, SIDE) + piece, F32),
        ],
        in_specs=[SMEM] * 4 + [ANY] * 3,
        out_specs=[VMEM] * 2,
        scratch_shapes=[pltpu.VMEM((CORES, SIDE, SIDE, SIDE, 2, rows, WIDTH), BF16) for *_, rows in PARTS]
        + [pltpu.VMEM((SIDE, SIDE, BLOCKS, rows, WIDTH), BF16) for *_, rows in PARTS]
        + [pltpu.VMEM((3, SIDE, BLOCKS, rows, WIDTH), BF16) for *_, rows in PARTS]
        + [pltpu.VMEM((SIDE, BLOCKS, rows, WIDTH), BF16) for *_, rows in PARTS]
        + [pltpu.VMEM((3, BLOCKS, rows, WIDTH), BF16) for *_, rows in PARTS]
        + [
            pltpu.VMEM((BLOCKS, ROWS, WIDTH), F32),
            pltpu.VMEM((3, SIDE, SIDE, SIDE) + piece, F32),
            pltpu.VMEM((3, SIDE, SIDE, SIDE) + piece, F32),
            pltpu.VMEM((3, SIDE, SIDE) + piece, F32),
            pltpu.VMEM((3, 3, SIDE, SIDE) + piece, F32),
            pltpu.VMEM((3, SIDE) + piece, F32),
            pltpu.VMEM((3, 3, SIDE) + piece, F32),
            pltpu.VMEM((3, 3) + piece, F32),
            dma((3, 7, SIDE)), dma((3, 7, SIDE)), dma((5,)),
            dma((3, 3, SIDE)), dma((3, 3, SIDE)), dma((3, 3)), dma((3, 3)),
            dma((4,)), dma((6, 3, 3)), dma((6, 3, 3)),
        ],
        compiler_params=pltpu.CompilerParams(collective_id=2, has_side_effects=True, vmem_limit_bytes=58 * MIB),
        name="return_grads",
    )(scale, *ids, grads, extra, terms)


def slot_specs(remote_steps):
    return [
        pl.BlockSpec((WIDE, ROWS, ROWS), lambda i: (jnp.minimum(i, remote_steps - 1), 0, 0)),
        pl.BlockSpec((WIDE, ROWS, ROWS), lambda i: (jnp.maximum(i - remote_steps, 0), 0, 0)),
    ]


def whole(shape):
    return pl.BlockSpec(shape, lambda i: (0,) * len(shape), pipeline_mode=pl.Buffered(1))


def degree_kernel(remote_steps, tgt, valid, remote_adj, local_adj, cot, scaled, norm, total):
    i = pl.program_id(0)

    @pl.when(i == 0)
    def _():
        total[...] = jnp.zeros_like(total)

    def add(adj):
        for l in range(WIDE):
            s = i * WIDE + l
            total[tgt[s]] += adj[l].astype(F32) * valid[s]

    @pl.when(i < remote_steps)
    def _():
        add(remote_adj)

    @pl.when(i >= remote_steps)
    def _():
        add(local_adj)

    @pl.when(i == pl.num_programs(0) - 1)
    def _():
        for t in range(BLOCKS):
            row_norm = lax.rsqrt(1.0 + jnp.sum(total[t], axis=1, keepdims=True))
            scaled[t] = (cot[t].astype(F32) * row_norm).astype(BF16)
            norm[t] = jnp.broadcast_to(row_norm, (ROWS, ROWS))


def degrees(tgt, valid, remote_adj, local_adj, cot):
    remote_steps, local_steps = remote_adj.shape[0] // WIDE, local_adj.shape[0] // WIDE
    return pl.pallas_call(
        functools.partial(degree_kernel, remote_steps),
        grid=(remote_steps + local_steps,),
        out_shape=[
            jax.ShapeDtypeStruct((BLOCKS, ROWS, WIDTH), BF16),
            jax.ShapeDtypeStruct((BLOCKS, ROWS, ROWS), F32),
        ],
        in_specs=[SMEM] * 2 + slot_specs(remote_steps) + [whole((BLOCKS, ROWS, WIDTH))],
        out_specs=[whole((BLOCKS, ROWS, WIDTH)), whole((BLOCKS, ROWS, ROWS))],
        scratch_shapes=[pltpu.VMEM((BLOCKS, ROWS, ROWS), F32)],
        compiler_params=pltpu.CompilerParams(vmem_limit_bytes=32 * MIB),
        name="degrees",
    )(tgt, valid, remote_adj, local_adj, cot)


def forward_kernel(
    remote_steps, tgt, rel, valid, src, coeffs, remote_adj, local_adj, incoming, feats, weights, scaled, cot, norm,
    self_weight, bases, out, terms, mixed, outer, held, inner,
):
    i = pl.program_id(0)

    @pl.when(i == 0)
    def _():
        mixed[...] = jnp.zeros_like(mixed)
        outer[...] = jnp.zeros_like(outer)

    def visit(adj, rows_of):
        for l in range(WIDE):
            rows = jnp.dot(adj[l], rows_of(l), preferred_element_type=F32)
            held[l] = (rows * valid[i * WIDE + l]).astype(BF16)
        for l in range(WIDE):
            s = i * WIDE + l
            mixed[tgt[s]] += jnp.dot(held[l], weights[rel[s]], preferred_element_type=F32)
            outer[rel[s]] += lax.dot_general(
                held[l], scaled[tgt[s]], (((0,), (0,)), ((), ())), preferred_element_type=F32
            )

    @pl.when(i < remote_steps)
    def _():
        visit(remote_adj, lambda l: incoming[l])

    @pl.when(i >= remote_steps)
    def _():
        visit(local_adj, lambda l: feats[src[(i - remote_steps) * WIDE + l]])

    @pl.when(i == pl.num_programs(0) - 1)
    def _():
        relations = outer.shape[0]
        basis_count = bases.shape[0]
        for t in range(BLOCKS):
            own = jnp.dot(feats[t], self_weight[...], preferred_element_type=F32)
            for half in range(2):
                cols = pl.ds(half * ROWS, ROWS)
                out[t, :, cols] = (
                    norm[t] * mixed[t, :, cols] + own[:, half * ROWS : (half + 1) * ROWS]
                ).astype(BF16)
        self_grad = jnp.zeros((WIDTH, WIDTH), F32)
        for t in range(BLOCKS):
            self_grad += lax.dot_general(feats[t], cot[t], (((0,), (0,)), ((), ())), preferred_element_type=F32)
        terms[pl.ds(basis_count * WIDTH, WIDTH), :] = self_grad

        def mix(n, _):
            for half in range(2):
                totals = [jnp.zeros((32, WIDTH), F32)] * 4
                for r in range(relations):
                    piece = outer[r, pl.ds(n * 32, 32), :]
                    totals = [totals[b] + coeffs[r, half * 4 + b] * piece for b in range(4)]
                for b in range(4):
                    terms[pl.ds((half * 4 + b) * WIDTH + n * 32, 32), :] = totals[b]
            return 0

        lax.fori_loop(0, WIDTH // 32, mix, 0)
        inner[...] = jnp.zeros_like(inner)

        def products(n, _):
            rows = pl.ds(n * 16, 16)
            pieces = [bases[b, rows, :].astype(F32) for b in range(basis_count)]
            for r in range(relations):
                piece = outer[r, rows, :]
                for b in range(basis_count):
                    both = piece * pieces[b]
                    both = both[:8] + both[8:]
                    inner[r * basis_count + b] += both[:, :ROWS] + both[:, ROWS:]
            return 0

        lax.fori_loop(0, WIDTH // 16, products, 0)
        coef_rows = pl.ds((basis_count + 1) * WIDTH, relations * basis_count)
        terms[coef_rows, pl.ds(0, ROWS)] = jnp.sum(inner[...], axis=1)
        terms[coef_rows, pl.ds(ROWS, ROWS)] = jnp.zeros((relations * basis_count, ROWS), F32)
        used = (basis_count + 1) * WIDTH + relations * basis_count
        terms[pl.ds(used, TERMS - used), :] = jnp.zeros((TERMS - used, WIDTH), F32)


def forward_slots(
    tgt, rel, valid, src, coeffs, remote_adj, local_adj, incoming, feats, weights, scaled, cot, norm, self_weight, bases
):
    remote_steps, local_steps = remote_adj.shape[0] // WIDE, local_adj.shape[0] // WIDE
    relations, basis_count = coeffs.shape
    return pl.pallas_call(
        functools.partial(forward_kernel, remote_steps),
        grid=(remote_steps + local_steps,),
        out_shape=[
            jax.ShapeDtypeStruct((BLOCKS, ROWS, WIDTH), BF16),
            jax.ShapeDtypeStruct((TERMS, WIDTH), F32),
        ],
        in_specs=[SMEM] * 5
        + slot_specs(remote_steps)
        + [pl.BlockSpec((WIDE, ROWS, WIDTH), lambda i: (jnp.minimum(i, remote_steps - 1), 0, 0))]
        + [whole(a.shape) for a in (feats, weights, scaled, cot, norm, self_weight, bases)],
        out_specs=[whole((BLOCKS, ROWS, WIDTH)), whole((TERMS, WIDTH))],
        scratch_shapes=[
            pltpu.VMEM((BLOCKS, ROWS, WIDTH), F32),
            pltpu.VMEM((relations, WIDTH, WIDTH), F32),
            pltpu.VMEM((WIDE, ROWS, WIDTH), BF16),
            pltpu.VMEM((relations * basis_count, 8, ROWS), F32),
        ],
        compiler_params=pltpu.CompilerParams(vmem_limit_bytes=48 * MIB),
        name="forward_slots",
    )(tgt, rel, valid, src, coeffs, remote_adj, local_adj, incoming, feats, weights, scaled, cot, norm, self_weight, bases)


def local(
    node_feats, send_block, recv_block, recv_rel, recv_count, recv_adj, local_src, local_tgt, local_rel, local_adj,
    bases, coeffs, self_weight, cotangent,
):
    peers = lax.axis_size(("src", "tgt"))
    slot_cap = send_block.shape[2]
    remote_slots = peers * slot_cap
    relations, basis_count = coeffs.shape
    feats = node_feats.reshape(BLOCKS, ROWS, WIDTH)
    cot = cotangent.reshape(BLOCKS, ROWS, WIDTH)
    remote_adj = recv_adj.reshape(remote_slots, ROWS, ROWS)
    own_adj = local_adj[0]
    src = local_src[0]
    tgt = jnp.concatenate([recv_block.reshape(remote_slots), local_tgt[0]])
    rel = jnp.concatenate([recv_rel.reshape(remote_slots), local_rel[0]])
    remote_valid = (jnp.arange(slot_cap, dtype=jnp.int32)[None, :] < recv_count[0][:, None]).astype(F32)
    valid = jnp.concatenate([remote_valid.reshape(remote_slots), jnp.ones((src.shape[0],), F32)])
    wide_coeffs = coeffs.astype(F32)
    scaled, norm = degrees(tgt, valid, remote_adj, own_adj, cot)
    *gathered, weights, extra, grads = gather_plane(
        wide_coeffs, tgt, rel, valid, src, feats, send_block[0].T, bases, scaled, cot, self_weight, remote_adj, own_adj
    )
    gathered, ids = gathered[:3], gathered[3:]
    incoming = exchange_picks(gathered, ids).reshape(remote_slots, ROWS, WIDTH)
    features_out, terms = forward_slots(
        tgt, rel, valid, src, wide_coeffs, remote_adj, own_adj, incoming, feats, weights, scaled, cot, norm,
        self_weight, bases,
    )
    scale = jnp.full((1,), 1.0 / math.sqrt(node_feats.shape[0] * peers), F32)
    grad_features, totals = return_grads(
        scale,
        ids,
        grads.reshape(SIDE, CORES, SIDE, SIDE, slot_cap, ROWS, WIDTH),
        extra,
        terms.reshape(CORES, 3, SIDE, SIDE, SIDE, TERM_ROWS, WIDTH),
    )
    totals = totals.reshape(TERMS, WIDTH)
    basis_rows = basis_count * WIDTH
    return (
        features_out.reshape(node_feats.shape),
        grad_features.reshape(node_feats.shape),
        totals[:basis_rows].reshape(basis_count, WIDTH, WIDTH),
        jnp.sum(totals[basis_rows + WIDTH : basis_rows + WIDTH + relations * basis_count], axis=1).reshape(relations, basis_count),
        totals[basis_rows : basis_rows + WIDTH],
    )


def solution(mesh):
    both = ("src", "tgt")
    in_specs = (
        P(both, None),
        P(both, None, None),
        P(both, None, None),
        P(both, None, None),
        P(both, None),
        P(both, None, None, None, None),
        P(both, None),
        P(both, None),
        P(both, None),
        P(both, None, None, None),
        P(),
        P(),
        P(),
        P(both, None),
    )
    out_specs = (P(both, None), P(both, None), P(), P(), P())
    return jax.shard_map(local, mesh=mesh, in_specs=in_specs, out_specs=out_specs, check_vma=False)
```

```python
import functools
import math

import jax
import jax.numpy as jnp
from jax import lax
from jax.experimental import pallas as pl
from jax.experimental.pallas import tpu as pltpu
from jax.sharding import PartitionSpec as P

MESH = pl.DeviceIdType.MESH
MIB = 1 << 20
F32 = jnp.float32
BF16 = jnp.bfloat16
SIDE = 4
CORES = 2
BLOCKS = 8
ROWS = 128
WIDTH = 256
STEP = 8
WIDE = 32
PIECES = 4
CHUNKS = 8
TERM_ROWS = 8
PARTS = (("x", "y", "z", 0, 48), ("y", "z", "x", 48, 48), ("z", "x", "y", 96, 32))
AXES = ("y", "z", "x")
HOPS = (1, 3, 2)
ANY = pl.BlockSpec(memory_space=pl.ANY)
VMEM = pl.BlockSpec(memory_space=pltpu.VMEM)
SMEM = pl.BlockSpec(memory_space=pltpu.SMEM)


def place():
    src, tgt = lax.axis_index("src"), lax.axis_index("tgt")
    return {"y": src // CORES, "c": src % CORES, "z": tgt // SIDE, "x": tgt % SIDE}


def device(at):
    return (at["y"] * CORES + at["c"], at["z"] * SIDE + at["x"])


def band(at):
    return (at["y"] * CORES + at["c"]) * SIDE * SIDE + at["z"] * SIDE + at["x"]


def moved(me, axis, hop):
    return {**me, axis: (me[axis] + hop) % SIDE}


def line_peers(me, axis):
    peers = []
    for hop in HOPS:
        for flip in (0, 1):
            peers.append((hop, flip, {**moved(me, axis, hop), "c": (me["c"] + flip) % CORES}))
    peers.append((0, 1, {**me, "c": (me["c"] + 1) % CORES}))
    return peers


def greet(peers):
    barrier = pltpu.get_barrier_semaphore()
    for peer in peers:
        pl.semaphore_signal(barrier, inc=1, device_id=device(peer), device_id_type=MESH)
    pl.semaphore_wait(barrier, len(peers))


def plane_dims(last):
    return tuple(a for a in AXES if a != last)


def plane_at(ref, last, **where):
    return ref.at[tuple(where.get(a, slice(None)) for a in plane_dims(last))]


def band_at(ref, core, row, rows, **where):
    where = {"y": slice(None), "z": slice(None), "x": slice(None), **where}
    return ref.at[where["y"], core, where["z"], where["x"], :, pl.ds(row, rows), :]


def remote(src, dst, send, recv, peer):
    return pltpu.make_async_remote_copy(
        src_ref=src, dst_ref=dst, send_sem=send, recv_sem=recv, device_id=device(peer), device_id_type=MESH
    )


def spread_kernel(
    coeffs, recv_tgt, recv_rel, recv_count, local_tgt, local_rel, src, feats, picks, bases, scaled, cot, self_weight, remote_adj, local_adj,
    incoming, i0, i1, i2, weights, extra, grads, self_out, self_grad,
    feats_here, *refs,
):
    gathered, refs = (refs[0:4], refs[4:8], refs[8:12]), refs[12:]
    (
        t0, t1, t2, b0, b1, b2, adj, own_adj, cots, staged, part,
        own_sem, adj_sem, out_sem, is1, ir1, is2, ir2, table_sem, gs1, gr1, gs2, gr2, send, recv, self_sem,
    ) = refs
    me = place()
    ids, tables, packed = (i0, i1, i2), (t0, t1, t2), (b0, b1, b2)
    relations, remote_slots, local_slots = cots.shape[0], adj.shape[0], own_adj.shape[0]
    chunk = remote_slots // CHUNKS
    partner = {**me, "c": (me["c"] + 1) % CORES}
    adj_copies = [
        pltpu.make_async_copy(remote_adj, adj, adj_sem.at[0]),
        pltpu.make_async_copy(local_adj, own_adj, adj_sem.at[1]),
        pltpu.make_async_copy(feats, feats_here, adj_sem.at[2]),
    ]
    own = []
    for j, (a1, a2, last, row, rows) in enumerate(PARTS):
        here = {a1: me[a1], a2: me[a2]}
        own.append(
            pltpu.make_async_copy(feats.at[:, pl.ds(row, rows), :], gathered[j][0].at[me[a1]], own_sem.at[j, 0])
        )
        own.append(pltpu.make_async_copy(picks, plane_at(ids[j], last, **here), own_sem.at[j, 1]))
    for copy in own + adj_copies:
        copy.start()
    greet([p for axis in AXES for hop, flip, p in line_peers(me, axis) if hop] + [partner])

    def begin(copies):
        for copy in copies:
            copy.start()
        return copies

    def done(copies):
        for copy in copies:
            copy.wait()

    def column(j, e, far=0):
        return gathered[j][far].at[(me[PARTS[j][0]] + e) % SIDE]

    ids_first = begin(
        [
            remote(
                picks, plane_at(ids[j], last, **{a1: me[a1], a2: me[a2]}), is1.at[j, h - 1], ir1.at[j, h - 1],
                moved(me, a1, h),
            )
            for h in HOPS
            for j, (a1, a2, last, row, rows) in enumerate(PARTS)
        ]
    )
    first = {}
    for way, hop in enumerate((1, 3)):
        for j, (a1, a2, last, row, rows) in enumerate(PARTS):
            first[j, way, 0] = remote(
                feats.at[:, pl.ds(row, rows), :], column(j, 0), gs1.at[j, way, 0], gr1.at[j, way, 0],
                moved(me, a1, hop),
            )
            first[j, way, 0].start()
    done(ids_first)
    done([own[1], own[3], own[5]])
    ids_rest = begin(
        [
            remote(
                plane_at(ids[j], last, **{a2: me[a2]}), plane_at(ids[j], last, **{a2: me[a2]}),
                is2.at[j, h - 1], ir2.at[j, h - 1], moved(me, a2, h),
            )
            for h in HOPS
            for j, (a1, a2, last, row, rows) in enumerate(PARTS)
        ]
    )
    second = {}

    def onward(e):
        for way, hop in enumerate((1, 3)):
            for j, (a1, a2, last, row, rows) in enumerate(PARTS):
                from_ = column(j, e) if e else feats.at[:, pl.ds(row, rows), :]
                second[j, e, way, 0] = remote(
                    from_, column(j, e, (3, 1)[way]), gs2.at[j, e, way, 0], gr2.at[j, e, way, 0], moved(me, a2, hop)
                )
                second[j, e, way, 0].start()

    onward(0)

    def mix(r, _):
        for n in range(8):
            rows = pl.ds(n * 32, 32)
            total = coeffs[r, 0] * bases[0, rows, :].astype(F32)
            for b in range(1, 8):
                total = total + coeffs[r, b] * bases[b, rows, :].astype(F32)
            weights[r, rows, :] = total.astype(BF16)
        for t in range(BLOCKS):
            cots[r, t] = lax.dot_general(
                scaled[t], weights[r], (((1,), (1,)), ((), ())), preferred_element_type=F32
            ).astype(BF16)
        return 0

    def relay_first(way):
        hop = (1, 3)[way]
        e = (3, 1)[way]
        for j, part_of in enumerate(PARTS):
            first[j, way, 0].wait_recv()
            half = column(j, e).at[pl.ds(way * 4, 4)]
            first[j, way, 1] = remote(half, half, gs1.at[j, way, 1], gr1.at[j, way, 1], moved(me, part_of[0], hop))
            first[j, way, 1].start()

    def relay_second(e):
        for way, hop in enumerate((1, 3)):
            for j, part_of in enumerate(PARTS):
                second[j, e, way, 0].wait_recv()
                half = pl.ds(way * 4, 4)
                second[j, e, way, 1] = remote(
                    column(j, e, (3, 1)[way]).at[half], column(j, e, 2).at[half], gs2.at[j, e, way, 1], gr2.at[j, e, way, 1], moved(me, part_of[1], hop)
                )
                second[j, e, way, 1].start()

    lines = {}

    def exchange(group, slot):
        lines[group] = []
        for n in range(8):
            for j, (a1, a2, last, row, rows) in enumerate(PARTS):
                peer = me if n == 7 else line_peers(me, last)[n][2]
                owner = band(peer)
                far = (me[a2] + group) % SIDE

                def one(k, _, j=j, n=n, a1=a1, a2=a2, last=last, owner=owner, far=far):
                    where = {a1: k, a2: far}
                    spot = tuple(where[a] for a in plane_dims(last))
                    for c in range(2):
                        packed[j][slot, n, k, c] = gathered[j][group][k, tables[j][spot + (c, owner)]]
                    return 0

                lax.fori_loop(0, SIDE, one, 0)
                target = band_at(incoming, me["c"], row, rows, **{last: me[last], a2: far})
                if n == 7:
                    copy = pltpu.make_async_copy(packed[j].at[slot, n], target, self_sem.at[j, group])
                else:
                    copy = remote(packed[j].at[slot, n], target, send.at[j, n, group], recv.at[j, n, group], peer)
                copy.start()
                lines[group].append(copy)

    def free(group):
        for copy in lines[group][:21]:
            copy.wait_send()
        for copy in lines[group][21:]:
            copy.wait()

    def slot_chunk(k):
        return pltpu.make_async_copy(staged.at[k % 2], grads.at[pl.ds(k * chunk, chunk)], out_sem.at[k])

    def slot_grads(low, high):
        for k in range(low, high):
            if k >= 2:
                slot_chunk(k - 2).wait()

            def group(g, _, k=k):
                for l in range(STEP):
                    peer, c = (k * chunk + g * STEP) // 2 + l // 2, l % 2
                    grad = lax.dot_general(
                        adj[2 * peer + c],
                        cots[recv_rel[c, peer], recv_tgt[c, peer]],
                        (((0,), (0,)), ((), ())),
                        preferred_element_type=F32,
                    )
                    valid = (c < recv_count[0, peer]).astype(F32)
                    staged[k % 2, g * STEP + l] = (grad * valid).astype(BF16)
                return 0

            lax.fori_loop(0, chunk // STEP, group, 0)
            slot_chunk(k).start()

    lax.fori_loop(0, 6, mix, 0)
    relay_first(0)
    relay_first(1)
    onward(3)
    onward(1)
    done(ids_rest)
    loads = begin([pltpu.make_async_copy(ids[j], tables[j], table_sem.at[j]) for j in range(3)])
    lax.fori_loop(6, 14, mix, 0)
    for j in range(3):
        for way in range(2):
            first[j, way, 1].wait_recv()
    onward(2)
    done(loads)
    done([own[0], own[2], own[4]])
    exchange(0, 0)
    relay_second(0)
    lax.fori_loop(14, 22, mix, 0)
    relay_second(3)
    relay_second(1)
    lax.fori_loop(22, relations, mix, 0)
    relay_second(2)
    exchange(1, 1)
    done(adj_copies)
    slot_grads(0, 2)
    free(0)
    exchange(3, 0)
    slot_grads(2, 4)
    for e in range(SIDE):
        for j in range(3):
            for way in range(2):
                second[j, e, way, 1].wait_recv()
    free(1)
    exchange(2, 1)
    slot_grads(4, CHUNKS)
    for t in range(BLOCKS):
        extra[t] = lax.dot_general(cot[t], self_weight[...], (((1,), (1,)), ((), ())), preferred_element_type=F32)

    def local_group(g, _):
        for l in range(STEP):
            s = g * STEP + l
            part[l] = lax.dot_general(
                own_adj[s], cots[local_rel[0, s], local_tgt[0, s]], (((0,), (0,)), ((), ())),
                preferred_element_type=F32,
            ).astype(BF16)
        for k in range(BLOCKS):
            hits = [(src[0, g * STEP + l] == k).astype(F32) for l in range(STEP)]
            for n in range(4):
                rows = pl.ds(n * 32, 32)
                total = extra[k, rows, :]
                for l in range(STEP):
                    total = total + hits[l] * part[l, rows, :].astype(F32)
                extra[k, rows, :] = total
        return 0

    lax.fori_loop(0, local_slots // STEP, local_group, 0)
    total = jnp.zeros((WIDTH, WIDTH), F32)
    for t in range(BLOCKS):
        self_out[t] = jnp.dot(feats_here[t], self_weight[...], preferred_element_type=F32)
        total += lax.dot_general(feats_here[t], cot[t], (((0,), (0,)), ((), ())), preferred_element_type=F32)
    self_grad[...] = total
    slot_chunk(CHUNKS - 2).wait()
    slot_chunk(CHUNKS - 1).wait()
    for copy in list(first.values()) + list(second.values()):
        copy.wait_send()
    free(3)
    free(2)
    for group in range(SIDE):
        for copy in lines[group][:21]:
            copy.wait_recv()


def spread_features(coeffs, slots, feats, picks, bases, scaled, cot, self_weight, remote_adj, local_adj):
    relations, remote_slots = coeffs.shape[0], remote_adj.shape[0]
    dma = pltpu.SemaphoreType.DMA
    return pl.pallas_call(
        spread_kernel,
        out_shape=[jax.ShapeDtypeStruct((SIDE, CORES, SIDE, SIDE, 2, ROWS, WIDTH), BF16)]
        + [jax.ShapeDtypeStruct((SIDE, SIDE) + picks.shape, jnp.int32)] * 3
        + [
            jax.ShapeDtypeStruct((relations, WIDTH, WIDTH), BF16),
            jax.ShapeDtypeStruct((BLOCKS, ROWS, WIDTH), F32),
            jax.ShapeDtypeStruct((remote_slots, ROWS, WIDTH), BF16),
            jax.ShapeDtypeStruct((BLOCKS, ROWS, WIDTH), F32),
            jax.ShapeDtypeStruct((WIDTH, WIDTH), F32),
        ],
        in_specs=[SMEM] * 7 + [ANY] * 2 + [VMEM] * 4 + [ANY] * 2,
        out_specs=[ANY] * 4 + [VMEM] * 2 + [ANY] + [VMEM] * 2,
        scratch_shapes=[pltpu.VMEM((BLOCKS, ROWS, WIDTH), BF16)]
        + [pltpu.VMEM((SIDE, BLOCKS, rows, WIDTH), BF16) for *_, rows in PARTS for _ in range(SIDE)]
        + [pltpu.SMEM((SIDE, SIDE) + picks.shape, jnp.int32)] * 3
        + [pltpu.VMEM((2, 8, SIDE, 2, rows, WIDTH), BF16) for *_, rows in PARTS]
        + [
            pltpu.VMEM(remote_adj.shape, BF16),
            pltpu.VMEM(local_adj.shape, BF16),
            pltpu.VMEM((relations, BLOCKS, ROWS, WIDTH), BF16),
            pltpu.VMEM((2, remote_slots // CHUNKS, ROWS, WIDTH), BF16),
            pltpu.VMEM((STEP, ROWS, WIDTH), BF16),
            dma((3, 2)), dma((3,)), dma((CHUNKS,)),
            dma((3, 3)), dma((3, 3)), dma((3, 3)), dma((3, 3)), dma((3,)),
            dma((3, 2, 2)), dma((3, 2, 2)), dma((3, SIDE, 2, 2)), dma((3, SIDE, 2, 2)),
            dma((3, 7, SIDE)), dma((3, 7, SIDE)), dma((3, SIDE)),
        ],
        compiler_params=pltpu.CompilerParams(collective_id=0, has_side_effects=True, vmem_limit_bytes=58 * MIB),
        name="spread_features",
    )(coeffs, *slots, feats, picks, bases, scaled, cot, self_weight, remote_adj, local_adj)


def return_kernel(
    coeffs, i0, i1, i2, grads, extra, outer_in, bases_in, self_grad, out, full, rest,
    r0, r1, r2, p0, p1, p2, l0, l1, l2, e0, e1, e2, q0, q1, q2, f0, f1, f2, added, outer, bases, inner, terms,
    wire, b0, b1, h1, b2, h2, b3, total,
    send, recv, own_sem, es, ev, ls, lv, s2, v2, pair_sem, ws, wr,
):
    me = place()
    ids, returned, sums, landed = (i0, i1, i2), (r0, r1, r2), (p0, p1, p2), (l0, l1, l2)
    early, held, final = (e0, e1, e2), (q0, q1, q2), (f0, f1, f2)
    core, partner = me["c"], {**me, "c": (me["c"] + 1) % CORES}
    relations, basis_count = coeffs.shape
    own = [
        pltpu.make_async_copy(outer_in, outer, own_sem.at[3]),
        pltpu.make_async_copy(bases_in, bases, own_sem.at[4]),
        pltpu.make_async_copy(self_grad, terms.at[2, 0, pl.ds(0, 2)], own_sem.at[5]),
        pltpu.make_async_copy(extra, added, own_sem.at[6]),
    ]
    for j, (a1, a2, last, row, rows) in enumerate(PARTS):
        own.append(
            pltpu.make_async_copy(
                band_at(grads, core, row, rows, **{last: me[last]}), returned[j].at[core, me[last]], own_sem.at[j]
            )
        )
    for copy in own:
        copy.start()
    greet([p for axis in AXES for hop, flip, p in line_peers(me, axis) if hop] + [partner])
    sent = [[], [], [], []]

    def give(group):
        for n in range(7):
            for j, (a1, a2, last, row, rows) in enumerate(PARTS):
                hop, flip, peer = line_peers(me, last)[n]
                far = (me[a2] + group) % SIDE
                copy = remote(
                    band_at(grads, peer["c"], row, rows, **{last: peer[last], a2: far}),
                    plane_at(returned[j].at[core, me[last]], last, **{a2: far}),
                    send.at[j, n, group],
                    recv.at[j, n, group],
                    peer,
                )
                copy.start()
                sent[group].append(copy)

    def weigh(stage, level, src, dst):
        copies = []
        for hop in HOPS:
            for j, part in enumerate(PARTS):
                axis = part[level]
                copy = remote(
                    src(j, (me[axis] + hop) % SIDE),
                    dst(j, hop - 1),
                    ws.at[stage, j, hop - 1],
                    wr.at[stage, j, hop - 1],
                    moved(me, axis, hop),
                )
                copy.start()
                copies.append(copy)
        return copies

    def done(copies):
        for copy in copies:
            copy.wait()

    def weight_terms():
        terms[2, 0, 2:4] = jnp.zeros((2, SIDE, SIDE, TERM_ROWS, WIDTH), F32)
        terms[2, 1] = jnp.zeros((SIDE, SIDE, SIDE, TERM_ROWS, WIDTH), F32)
        done(own[:3])

        def mix(n, _):
            for half in range(2):
                totals = [jnp.zeros((32, WIDTH), F32)] * 4
                for r in range(relations):
                    slab = outer[r, pl.ds(n * 32, 32), :]
                    totals = [totals[b] + coeffs[r, half * 4 + b] * slab for b in range(4)]
                for b in range(4):
                    terms[half, b // 2, (b % 2) * 2 + n // 4, n % 4] = totals[b].reshape(4, TERM_ROWS, WIDTH)
            return 0

        lax.fori_loop(0, WIDTH // 32, mix, 0)
        inner[...] = jnp.zeros_like(inner)

        def products(n, _):
            rows = pl.ds(n * 16, 16)
            slabs = [bases[b, rows, :].astype(F32) for b in range(basis_count)]
            for r in range(relations):
                slab = outer[r, rows, :]
                for b in range(basis_count):
                    both = slab * slabs[b]
                    both = both[:8] + both[8:]
                    inner[r * basis_count + b] += both[:, :ROWS] + both[:, ROWS:]
            return 0

        lax.fori_loop(0, WIDTH // 16, products, 0)
        for r in range(relations):
            terms[2, 0, 2 + r // 16, (r // 4) % 4, r % 4, :, pl.ds(0, ROWS)] = jnp.sum(
                inner[pl.ds(r * basis_count, basis_count)], axis=1
            )

    def piece(j, depth):
        spot = tuple(me[PARTS[j][level]] for level in (2, 1, 0)[:depth])
        return total.at[(j, core) + spot]

    def add(*parts):
        return sum(part.astype(F32) for part in parts[1:]) + parts[0].astype(F32)

    def spot_of(j, group, k):
        a1, a2, last, row, rows = PARTS[j]
        where = {a1: k, a2: (me[a2] + group) % SIDE}
        return tuple(where[a] for a in plane_dims(last))

    def fold(j, group, k, low, high, way=None):
        a1, a2, last, row, rows = PARTS[j]
        spot = spot_of(j, group, k)

        def two(n, _):
            if way is None:
                totals = [jnp.zeros((rows, WIDTH), F32)] * 2
            else:
                totals = [early[j][way, k, 2 * n + h - low].astype(F32) for h in range(2)]
            for other in range(CORES):
                for place_on in range(SIDE):
                    owner = band({**me, "c": other, last: place_on})
                    for c in range(2):
                        block = ids[j][spot + (c, owner)]
                        grad = returned[j][(other, place_on) + spot + (c,)].astype(F32)
                        totals = [totals[h] + (block == 2 * n + h).astype(F32) * grad for h in range(2)]
            for h in range(2):
                sums[j][spot + (2 * n + h,)] = totals[h].astype(BF16)
            return 0

        lax.fori_loop(low // 2, high // 2, two, 0)

    def half_on(j, way, k):
        return remote(
            sums[j].at[spot_of(j, 2, k) + (pl.ds(way * 4, 4),)], early[j].at[way, k], es.at[j, way, k],
            ev.at[j, way, k], moved(me, PARTS[j][1], (1, 3)[way]),
        )

    def across(j, way, late, k):
        low = 4 * way if late else 4 - 4 * way
        return remote(
            sums[j].at[spot_of(j, (1, 3)[way], k) + (pl.ds(low, 4),)], landed[j].at[way, k, pl.ds(low, 4)],
            ls.at[j, way, late, k], lv.at[j, way, late, k], moved(me, PARTS[j][1], (1, 3)[way]),
        )

    def each_band(work):
        def one(k, _):
            for j in range(3):
                work(j, k)
            return 0

        lax.fori_loop(0, SIDE, one, 0)

    def far_bands(j, k):
        fold(j, 2, k, 0, BLOCKS)
        half_on(j, 0, k).start()
        half_on(j, 1, k).start()

    def near_bands(way, late):
        def work(j, k):
            low = 4 * way if late else 4 - 4 * way
            if late:
                half_on(j, way, k).wait()
            fold(j, (1, 3)[way], k, low, low + 4, way if late else None)
            across(j, way, late, k).start()

        return work

    give(2)
    give(1)
    weight_terms()
    for j in range(3):
        for c in range(CORES):
            for k in range(SIDE):
                slab = terms[j, c, k]
                wire[j, c, k] = jnp.concatenate([slab[..., :ROWS], slab[..., ROWS:]], axis=2).astype(BF16)
    halves = remote(wire.at[:, partner["c"]], b0, pair_sem.at[0], pair_sem.at[1], partner)
    halves.start()
    give(3)
    done(own[3:])
    done(sent[2])
    each_band(far_bands)
    halves.wait()
    b0[...] = add(wire[:, core], b0[...]).astype(BF16)
    stage = weigh(0, 2, lambda j, k: b0.at[j, k], lambda j, h: b1.at[j, h])
    give(0)
    done(sent[1])
    each_band(near_bands(0, 0))
    done(stage)
    for j, part in enumerate(PARTS):
        h1[j] = add(b0[j, me[part[2]]], b1[j, 0], b1[j, 1], b1[j, 2]).astype(BF16)
    stage = weigh(1, 1, lambda j, k: h1.at[j, k], lambda j, h: b2.at[j, h])
    done(sent[3])
    each_band(near_bands(1, 0))
    done(stage)
    for j, part in enumerate(PARTS):
        h2[j] = add(h1[j, me[part[1]]], b2[j, 0], b2[j, 1], b2[j, 2]).astype(BF16)
    stage = weigh(2, 0, lambda j, k: h2.at[j, k], lambda j, h: b3.at[j, h])
    each_band(near_bands(0, 1))
    each_band(near_bands(1, 1))
    done(stage)
    for j, part in enumerate(PARTS):
        piece(j, 3)[...] = add(h2[j, me[part[0]]], b3[j, 0], b3[j, 1], b3[j, 2]).astype(BF16)
    stage = weigh(3, 0, lambda j, k: piece(j, 3), lambda j, h: piece(j, 3))
    done(sent[0])
    each_band(lambda j, k: fold(j, 0, k, 0, BLOCKS))
    done(stage)
    stage = weigh(4, 1, lambda j, k: piece(j, 2), lambda j, h: piece(j, 2))
    for j in range(3):
        for way in range(2):
            for late in range(2):
                for k in range(SIDE):
                    across(j, way, late, k).wait()
    second = []
    for hop in HOPS + (0,):
        for j, (a1, a2, last, row, rows) in enumerate(PARTS):
            k = (me[a1] + hop) % SIDE
            mine = sums[j].at[spot_of(j, 0, k)]

            def join(n, _, j=j, k=k, hop=hop, mine=mine):
                both = mine[n].astype(F32) + landed[j][0, k, n].astype(F32) + landed[j][1, k, n].astype(F32)
                held[j][hop, n] = both.astype(BF16)
                return 0

            lax.fori_loop(0, BLOCKS, join, 0)
            if hop:
                copy = remote(
                    held[j].at[hop], final[j].at[hop - 1], s2.at[j, hop - 1], v2.at[j, hop - 1], moved(me, a1, hop)
                )
                copy.start()
                second.append(copy)
    done(stage)
    stage = weigh(5, 2, lambda j, k: piece(j, 1), lambda j, h: piece(j, 1))
    done(second)
    done(stage)
    back = remote(total.at[:, core], total.at[:, core], pair_sem.at[2], pair_sem.at[3], partner)
    back.start()
    for j, (a1, a2, last, row, rows) in enumerate(PARTS):

        def end(n, _, j=j, row=row, rows=rows):
            both = added[n, pl.ds(row, rows), :] + held[j][0, n].astype(F32)
            for h in range(3):
                both = both + final[j][h, n].astype(F32)
            out[n, pl.ds(row, rows), :] = both.astype(BF16)
            return 0

        lax.fori_loop(0, BLOCKS, end, 0)
    back.wait()
    for j in range(3):
        ref = full.at[j] if j < 2 else rest.at[0]
        for c in range(CORES):
            for k in range(SIDE):
                slab = total[j, c, k].astype(F32)
                ref[c, k, :, :, :, pl.ds(0, ROWS)] = slab[:, :, :TERM_ROWS]
                ref[c, k, :, :, :, pl.ds(ROWS, ROWS)] = slab[:, :, TERM_ROWS:]


def return_grads(coeffs, ids, grads, extra, outer, bases, self_grad):
    dma = pltpu.SemaphoreType.DMA
    piece, packed = (TERM_ROWS, WIDTH), (2 * TERM_ROWS, ROWS)
    relations, basis_count = coeffs.shape
    return pl.pallas_call(
        return_kernel,
        out_shape=[
            jax.ShapeDtypeStruct((BLOCKS, ROWS, WIDTH), BF16),
            jax.ShapeDtypeStruct((2, CORES, SIDE, SIDE, SIDE) + piece, F32),
            jax.ShapeDtypeStruct((1, CORES, SIDE, SIDE, SIDE) + piece, F32),
        ],
        in_specs=[SMEM] * 4 + [ANY] * 5,
        out_specs=[VMEM] * 3,
        scratch_shapes=[pltpu.VMEM((CORES, SIDE, SIDE, SIDE, 2, rows, WIDTH), BF16) for *_, rows in PARTS]
        + [pltpu.VMEM((SIDE, SIDE, BLOCKS, rows, WIDTH), BF16) for *_, rows in PARTS]
        + [pltpu.VMEM((2, SIDE, BLOCKS, rows, WIDTH), BF16) for *_, rows in PARTS]
        + [pltpu.VMEM((2, SIDE, BLOCKS // 2, rows, WIDTH), BF16) for *_, rows in PARTS]
        + [pltpu.VMEM((SIDE, BLOCKS, rows, WIDTH), BF16) for *_, rows in PARTS]
        + [pltpu.VMEM((3, BLOCKS, rows, WIDTH), BF16) for *_, rows in PARTS]
        + [
            pltpu.VMEM((BLOCKS, ROWS, WIDTH), F32),
            pltpu.VMEM(outer.shape, F32),
            pltpu.VMEM(bases.shape, BF16),
            pltpu.VMEM((relations * basis_count, 8, ROWS), F32),
            pltpu.VMEM((3, CORES, SIDE, SIDE, SIDE) + piece, F32),
            pltpu.VMEM((3, CORES, SIDE, SIDE, SIDE) + packed, BF16),
            pltpu.VMEM((3, SIDE, SIDE, SIDE) + packed, BF16),
            pltpu.VMEM((3, 3, SIDE, SIDE) + packed, BF16),
            pltpu.VMEM((3, SIDE, SIDE) + packed, BF16),
            pltpu.VMEM((3, 3, SIDE) + packed, BF16),
            pltpu.VMEM((3, SIDE) + packed, BF16),
            pltpu.VMEM((3, 3) + packed, BF16),
            pltpu.VMEM((3, CORES, SIDE, SIDE, SIDE) + packed, BF16),
            dma((3, 7, SIDE)), dma((3, 7, SIDE)), dma((7,)),
            dma((3, 2, SIDE)), dma((3, 2, SIDE)), dma((3, 2, 2, SIDE)), dma((3, 2, 2, SIDE)), dma((3, 3)), dma((3, 3)),
            dma((6,)), dma((6, 3, 3)), dma((6, 3, 3)),
        ],
        compiler_params=pltpu.CompilerParams(collective_id=2, has_side_effects=True, vmem_limit_bytes=60 * MIB),
        name="return_grads",
    )(coeffs, *ids, grads, extra, outer, bases, self_grad)


def piece_specs(steps, start, width):
    size = WIDE // PIECES

    def at(q):
        return lambda i: (jnp.clip(i - start, 0, steps - 1) * PIECES + q, 0, 0)

    return [
        pl.BlockSpec((size, ROWS, width), at(q)) for q in range(PIECES)
    ]


def slot_specs(remote_steps, local_steps):
    return piece_specs(remote_steps, 0, ROWS) + piece_specs(local_steps, remote_steps, ROWS)


def slot_of(pieces, l):
    return pieces[l // (WIDE // PIECES)][l % (WIDE // PIECES)]


def whole(shape):
    return pl.BlockSpec(shape, lambda i: (0,) * len(shape), pipeline_mode=pl.Buffered(1))


def slot_ids(remote, i, l, recv_tgt, recv_rel, recv_count, local_tgt, local_rel):
    if remote:
        peer, c = i * (WIDE // 2) + l // 2, l % 2
        return recv_tgt[c, peer], recv_rel[c, peer], (c < recv_count[0, peer]).astype(F32)
    return local_tgt[0, i * WIDE + l], local_rel[0, i * WIDE + l], 1.0


def degree_kernel(
    recv_tgt, recv_rel, recv_count, local_tgt, local_rel, src, remote_adj, local_adj, cot, scaled, norm,
    total, remote_here, local_here, sem,
):
    lists = (recv_tgt, recv_rel, recv_count, local_tgt, local_rel)
    pairs = ((remote_adj, remote_here), (local_adj, local_here))
    copies = []
    for from_, to in pairs:
        for n in range(from_.shape[0] // WIDE):
            part = pl.ds(n * WIDE, WIDE)
            copies.append(pltpu.make_async_copy(from_.at[part], to.at[part], sem.at[len(copies)]))
            copies[-1].start()
    total[...] = jnp.zeros_like(total)
    done = 0
    for remote_side, (from_, to) in enumerate(pairs):
        for n in range(from_.shape[0] // WIDE):
            copies[done].wait()
            done += 1
            for l in range(WIDE):
                t, r, valid = slot_ids(remote_side == 0, n, l, *lists)
                total[t] += to[n * WIDE + l].astype(F32) * valid
    for t in range(BLOCKS):
        row_norm = lax.rsqrt(1.0 + jnp.sum(total[t], axis=1, keepdims=True))
        scaled[t] = (cot[t].astype(F32) * row_norm).astype(BF16)
        norm[t] = jnp.broadcast_to(row_norm, (ROWS, ROWS))


def degrees(slots, remote_adj, local_adj, cot):
    parts = (remote_adj.shape[0] + local_adj.shape[0]) // WIDE
    return pl.pallas_call(
        degree_kernel,
        out_shape=[
            jax.ShapeDtypeStruct((BLOCKS, ROWS, WIDTH), BF16),
            jax.ShapeDtypeStruct((BLOCKS, ROWS, ROWS), F32),
        ],
        in_specs=[SMEM] * 6 + [ANY] * 2 + [VMEM],
        out_specs=[VMEM] * 2,
        scratch_shapes=[
            pltpu.VMEM((BLOCKS, ROWS, ROWS), F32),
            pltpu.VMEM(remote_adj.shape, BF16),
            pltpu.VMEM(local_adj.shape, BF16),
            pltpu.SemaphoreType.DMA((parts,)),
        ],
        compiler_params=pltpu.CompilerParams(vmem_limit_bytes=58 * MIB),
        name="degrees",
    )(*slots, remote_adj, local_adj, cot)


def forward_kernel(
    remote_steps, recv_tgt, recv_rel, recv_count, local_tgt, local_rel, src, *refs,
):
    remote_adj, local_adj, incoming = (refs[n * PIECES : (n + 1) * PIECES] for n in range(3))
    feats, weights, scaled, norm, self_out, out, outer, mixed, held = refs[3 * PIECES :]
    i = pl.program_id(0)
    lists = (recv_tgt, recv_rel, recv_count, local_tgt, local_rel)

    @pl.when(i == 0)
    def _():
        mixed[...] = jnp.zeros_like(mixed)
        outer[...] = jnp.zeros_like(outer)

    def visit(remote, step, adj, rows_of):
        for l in range(WIDE):
            t, r, valid = slot_ids(remote, step, l, *lists)
            held[l] = (jnp.dot(slot_of(adj, l), rows_of(l), preferred_element_type=F32) * valid).astype(BF16)
        for l in range(WIDE):
            t, r, valid = slot_ids(remote, step, l, *lists)
            mixed[t] += jnp.dot(held[l], weights[r], preferred_element_type=F32)
            outer[r] += lax.dot_general(held[l], scaled[t], (((0,), (0,)), ((), ())), preferred_element_type=F32)

    @pl.when(i < remote_steps)
    def _():
        visit(True, i, remote_adj, lambda l: slot_of(incoming, l))

    @pl.when(i >= remote_steps)
    def _():
        step = i - remote_steps
        visit(False, step, local_adj, lambda l: feats[src[0, step * WIDE + l]])

    @pl.when(i == pl.num_programs(0) - 1)
    def _():
        for t in range(BLOCKS):
            for half in range(2):
                cols = pl.ds(half * ROWS, ROWS)
                out[t, :, cols] = (norm[t] * mixed[t, :, cols] + self_out[t, :, cols]).astype(BF16)


def forward_slots(slots, remote_adj, local_adj, incoming, feats, weights, scaled, norm, self_out):
    remote_steps, local_steps = remote_adj.shape[0] // WIDE, local_adj.shape[0] // WIDE
    relations = weights.shape[0]
    return pl.pallas_call(
        functools.partial(forward_kernel, remote_steps),
        grid=(remote_steps + local_steps,),
        out_shape=[
            jax.ShapeDtypeStruct((BLOCKS, ROWS, WIDTH), BF16),
            jax.ShapeDtypeStruct((relations, WIDTH, WIDTH), F32),
        ],
        in_specs=[SMEM] * 6
        + slot_specs(remote_steps, local_steps)
        + piece_specs(remote_steps, 0, WIDTH)
        + [whole(a.shape) for a in (feats, weights, scaled, norm, self_out)],
        out_specs=[whole((BLOCKS, ROWS, WIDTH)), whole((relations, WIDTH, WIDTH))],
        scratch_shapes=[pltpu.VMEM((BLOCKS, ROWS, WIDTH), F32), pltpu.VMEM((WIDE, ROWS, WIDTH), BF16)],
        compiler_params=pltpu.CompilerParams(vmem_limit_bytes=58 * MIB),
        name="forward_slots",
    )(
        *slots, *[remote_adj] * PIECES, *[local_adj] * PIECES, *[incoming] * PIECES, feats, weights, scaled, norm,
        self_out,
    )


def local(
    node_feats, send_block, recv_block, recv_rel, recv_count, recv_adj, local_src, local_tgt, local_rel, local_adj,
    bases, coeffs, self_weight, cotangent,
):
    peers = lax.axis_size(("src", "tgt"))
    slot_cap = send_block.shape[2]
    remote_slots = peers * slot_cap
    relations, basis_count = coeffs.shape
    feats = node_feats.reshape(BLOCKS, ROWS, WIDTH)
    cot = cotangent.reshape(BLOCKS, ROWS, WIDTH)
    remote_adj = recv_adj.reshape(remote_slots, ROWS, ROWS)
    own_adj = local_adj[0]
    slots = (recv_block[0].T, recv_rel[0].T, recv_count, local_tgt, local_rel, local_src)
    wide_coeffs = coeffs.astype(F32)
    scaled, norm = degrees(slots, remote_adj, own_adj, cot)
    incoming, *ids, weights, extra, grads, self_out, self_grad = spread_features(
        wide_coeffs, slots, feats, send_block[0].T, bases, scaled, cot, self_weight, remote_adj, own_adj
    )
    incoming = incoming.reshape(remote_slots, ROWS, WIDTH)
    features_out, outer = forward_slots(slots, remote_adj, own_adj, incoming, feats, weights, scaled, norm, self_out)
    grad_features, grad_bases, rest = return_grads(
        wide_coeffs,
        ids,
        grads.reshape(SIDE, CORES, SIDE, SIDE, slot_cap, ROWS, WIDTH),
        extra,
        outer,
        bases,
        self_grad.reshape(2, SIDE, SIDE, TERM_ROWS, WIDTH),
    )
    scale = 1.0 / math.sqrt(node_feats.shape[0] * peers)
    rest = rest.reshape(-1, WIDTH)
    coef = rest[WIDTH : WIDTH + relations * basis_count, :ROWS]
    return (
        features_out.reshape(node_feats.shape),
        grad_features.reshape(node_feats.shape),
        grad_bases.reshape(bases.shape) * scale,
        jnp.sum(coef, axis=1).reshape(relations, basis_count) * scale,
        rest[:WIDTH] * scale,
    )


def solution(mesh):
    both = ("src", "tgt")
    in_specs = (
        P(both, None),
        P(both, None, None),
        P(both, None, None),
        P(both, None, None),
        P(both, None),
        P(both, None, None, None, None),
        P(both, None),
        P(both, None),
        P(both, None),
        P(both, None, None, None),
        P(),
        P(),
        P(),
        P(both, None),
    )
    out_specs = (P(both, None), P(both, None), P(), P(), P())
    return jax.shard_map(local, mesh=mesh, in_specs=in_specs, out_specs=out_specs, check_vma=False)
```

```python
import functools
import math

import jax
import jax.numpy as jnp
from jax import lax
from jax.experimental import pallas as pl
from jax.experimental.pallas import tpu as pltpu
from jax.sharding import PartitionSpec as P

MESH = pl.DeviceIdType.MESH
MIB = 1 << 20
F32 = jnp.float32
BF16 = jnp.bfloat16
SIDE = 4
CORES = 2
BLOCKS = 8
ROWS = 128
WIDTH = 256
STEP = 8
WIDE = 32
PIECES = 1
CHUNKS = 8
TERM_ROWS = 8
PARTS = (("x", "y", "z", 0, 48), ("y", "z", "x", 48, 48), ("z", "x", "y", 96, 32))
AXES = ("y", "z", "x")
HOPS = (1, 3, 2)
ANY = pl.BlockSpec(memory_space=pl.ANY)
VMEM = pl.BlockSpec(memory_space=pltpu.VMEM)
SMEM = pl.BlockSpec(memory_space=pltpu.SMEM)


def place():
    src, tgt = lax.axis_index("src"), lax.axis_index("tgt")
    return {"y": src // CORES, "c": src % CORES, "z": tgt // SIDE, "x": tgt % SIDE}


def device(at):
    return (at["y"] * CORES + at["c"], at["z"] * SIDE + at["x"])


def band(at):
    return (at["y"] * CORES + at["c"]) * SIDE * SIDE + at["z"] * SIDE + at["x"]


def moved(me, axis, hop):
    return {**me, axis: (me[axis] + hop) % SIDE}


def line_peers(me, axis):
    peers = []
    for hop in HOPS:
        for flip in (0, 1):
            peers.append((hop, flip, {**moved(me, axis, hop), "c": (me["c"] + flip) % CORES}))
    peers.append((0, 1, {**me, "c": (me["c"] + 1) % CORES}))
    return peers


def greet(peers):
    barrier = pltpu.get_barrier_semaphore()
    for peer in peers:
        pl.semaphore_signal(barrier, inc=1, device_id=device(peer), device_id_type=MESH)
    pl.semaphore_wait(barrier, len(peers))


def plane_dims(last):
    return tuple(a for a in AXES if a != last)


def plane_at(ref, last, **where):
    return ref.at[tuple(where.get(a, slice(None)) for a in plane_dims(last))]


def band_at(ref, core, row, rows, **where):
    where = {"y": slice(None), "z": slice(None), "x": slice(None), **where}
    return ref.at[where["y"], core, where["z"], where["x"], :, pl.ds(row, rows), :]


def remote(src, dst, send, recv, peer):
    return pltpu.make_async_remote_copy(
        src_ref=src, dst_ref=dst, send_sem=send, recv_sem=recv, device_id=device(peer), device_id_type=MESH
    )


def spread_kernel(
    coeffs, recv_tgt, recv_rel, recv_count, local_tgt, local_rel, src, feats, picks, bases, scaled, cot, self_weight, remote_adj, local_adj,
    incoming, i0, i1, i2, weights, extra, grads, self_out, self_grad,
    feats_here, *refs,
):
    gathered, refs = (refs[0:4], refs[4:8], refs[8:12]), refs[12:]
    (
        t0, t1, t2, b0, b1, b2, adj, own_adj, cots, staged, part,
        own_sem, adj_sem, out_sem, is1, ir1, is2, ir2, table_sem, gs1, gr1, gs2, gr2, send, recv, self_sem,
    ) = refs
    me = place()
    ids, tables, packed = (i0, i1, i2), (t0, t1, t2), (b0, b1, b2)
    relations, remote_slots, local_slots = cots.shape[0], adj.shape[0], own_adj.shape[0]
    chunk = remote_slots // CHUNKS
    partner = {**me, "c": (me["c"] + 1) % CORES}
    adj_copies = [
        pltpu.make_async_copy(remote_adj, adj, adj_sem.at[0]),
        pltpu.make_async_copy(local_adj, own_adj, adj_sem.at[1]),
        pltpu.make_async_copy(feats, feats_here, adj_sem.at[2]),
    ]
    own = []
    for j, (a1, a2, last, row, rows) in enumerate(PARTS):
        here = {a1: me[a1], a2: me[a2]}
        own.append(
            pltpu.make_async_copy(feats.at[:, pl.ds(row, rows), :], gathered[j][0].at[me[a1]], own_sem.at[j, 0])
        )
        own.append(pltpu.make_async_copy(picks, plane_at(ids[j], last, **here), own_sem.at[j, 1]))
    for copy in own + adj_copies:
        copy.start()
    greet([p for axis in AXES for hop, flip, p in line_peers(me, axis) if hop] + [partner])

    def begin(copies):
        for copy in copies:
            copy.start()
        return copies

    def done(copies):
        for copy in copies:
            copy.wait()

    def column(j, e, far=0):
        return gathered[j][far].at[(me[PARTS[j][0]] + e) % SIDE]

    ids_first = begin(
        [
            remote(
                picks, plane_at(ids[j], last, **{a1: me[a1], a2: me[a2]}), is1.at[j, h - 1], ir1.at[j, h - 1],
                moved(me, a1, h),
            )
            for h in HOPS
            for j, (a1, a2, last, row, rows) in enumerate(PARTS)
        ]
    )
    first = {}
    for way, hop in enumerate((1, 3)):
        for j, (a1, a2, last, row, rows) in enumerate(PARTS):
            first[j, way, 0] = remote(
                feats.at[:, pl.ds(row, rows), :], column(j, 0), gs1.at[j, way, 0], gr1.at[j, way, 0],
                moved(me, a1, hop),
            )
            first[j, way, 0].start()
    done(ids_first)
    done([own[1], own[3], own[5]])
    ids_rest = begin(
        [
            remote(
                plane_at(ids[j], last, **{a2: me[a2]}), plane_at(ids[j], last, **{a2: me[a2]}),
                is2.at[j, h - 1], ir2.at[j, h - 1], moved(me, a2, h),
            )
            for h in HOPS
            for j, (a1, a2, last, row, rows) in enumerate(PARTS)
        ]
    )
    second = {}

    def onward(e):
        for way, hop in enumerate((1, 3)):
            for j, (a1, a2, last, row, rows) in enumerate(PARTS):
                from_ = column(j, e) if e else feats.at[:, pl.ds(row, rows), :]
                second[j, e, way, 0] = remote(
                    from_, column(j, e, (3, 1)[way]), gs2.at[j, e, way, 0], gr2.at[j, e, way, 0], moved(me, a2, hop)
                )
                second[j, e, way, 0].start()

    onward(0)

    def mix(r, _):
        for n in range(8):
            rows = pl.ds(n * 32, 32)
            total = coeffs[r, 0] * bases[0, rows, :].astype(F32)
            for b in range(1, 8):
                total = total + coeffs[r, b] * bases[b, rows, :].astype(F32)
            weights[r, rows, :] = total.astype(BF16)
        for t in range(BLOCKS):
            cots[r, t] = lax.dot_general(
                scaled[t], weights[r], (((1,), (1,)), ((), ())), preferred_element_type=F32
            ).astype(BF16)
        return 0

    def relay_first(way):
        hop = (1, 3)[way]
        e = (3, 1)[way]
        for j, part_of in enumerate(PARTS):
            first[j, way, 0].wait_recv()
            half = column(j, e).at[pl.ds(way * 4, 4)]
            first[j, way, 1] = remote(half, half, gs1.at[j, way, 1], gr1.at[j, way, 1], moved(me, part_of[0], hop))
            first[j, way, 1].start()

    def relay_second(e):
        for way, hop in enumerate((1, 3)):
            for j, part_of in enumerate(PARTS):
                second[j, e, way, 0].wait_recv()
                half = pl.ds(way * 4, 4)
                second[j, e, way, 1] = remote(
                    column(j, e, (3, 1)[way]).at[half], column(j, e, 2).at[half], gs2.at[j, e, way, 1], gr2.at[j, e, way, 1], moved(me, part_of[1], hop)
                )
                second[j, e, way, 1].start()

    lines = {}

    def exchange(group, slot):
        lines[group] = []
        for n in range(8):
            for j, (a1, a2, last, row, rows) in enumerate(PARTS):
                peer = me if n == 7 else line_peers(me, last)[n][2]
                owner = band(peer)
                far = (me[a2] + group) % SIDE

                def one(k, _, j=j, n=n, a1=a1, a2=a2, last=last, owner=owner, far=far):
                    where = {a1: k, a2: far}
                    spot = tuple(where[a] for a in plane_dims(last))
                    for c in range(2):
                        packed[j][slot, n, k, c] = gathered[j][group][k, tables[j][spot + (c, owner)]]
                    return 0

                lax.fori_loop(0, SIDE, one, 0)
                target = band_at(incoming, me["c"], row, rows, **{last: me[last], a2: far})
                if n == 7:
                    copy = pltpu.make_async_copy(packed[j].at[slot, n], target, self_sem.at[j, group])
                else:
                    copy = remote(packed[j].at[slot, n], target, send.at[j, n, group], recv.at[j, n, group], peer)
                copy.start()
                lines[group].append(copy)

    def free(group):
        for copy in lines[group][:21]:
            copy.wait_send()
        for copy in lines[group][21:]:
            copy.wait()

    def slot_chunk(k):
        return pltpu.make_async_copy(staged.at[k % 2], grads.at[pl.ds(k * chunk, chunk)], out_sem.at[k])

    def slot_grads(low, high):
        for k in range(low, high):
            if k >= 2:
                slot_chunk(k - 2).wait()

            def group(g, _, k=k):
                for l in range(STEP):
                    peer, c = (k * chunk + g * STEP) // 2 + l // 2, l % 2
                    grad = lax.dot_general(
                        adj[2 * peer + c],
                        cots[recv_rel[c, peer], recv_tgt[c, peer]],
                        (((0,), (0,)), ((), ())),
                        preferred_element_type=F32,
                    )
                    valid = (c < recv_count[0, peer]).astype(F32)
                    staged[k % 2, g * STEP + l] = (grad * valid).astype(BF16)
                return 0

            lax.fori_loop(0, chunk // STEP, group, 0)
            slot_chunk(k).start()

    lax.fori_loop(0, 6, mix, 0)
    relay_first(0)
    relay_first(1)
    onward(3)
    onward(1)
    done(ids_rest)
    loads = begin([pltpu.make_async_copy(ids[j], tables[j], table_sem.at[j]) for j in range(3)])
    lax.fori_loop(6, 14, mix, 0)
    for j in range(3):
        for way in range(2):
            first[j, way, 1].wait_recv()
    onward(2)
    done(loads)
    done([own[0], own[2], own[4]])
    exchange(0, 0)
    relay_second(0)
    lax.fori_loop(14, 22, mix, 0)
    relay_second(3)
    relay_second(1)
    lax.fori_loop(22, relations, mix, 0)
    relay_second(2)
    exchange(1, 1)
    done(adj_copies)
    slot_grads(0, 2)
    free(0)
    exchange(3, 0)
    slot_grads(2, 4)
    for e in range(SIDE):
        for j in range(3):
            for way in range(2):
                second[j, e, way, 1].wait_recv()
    free(1)
    exchange(2, 1)
    slot_grads(4, CHUNKS)
    for t in range(BLOCKS):
        extra[t] = lax.dot_general(cot[t], self_weight[...], (((1,), (1,)), ((), ())), preferred_element_type=F32)

    def local_group(g, _):
        for l in range(STEP):
            s = g * STEP + l
            part[l] = lax.dot_general(
                own_adj[s], cots[local_rel[0, s], local_tgt[0, s]], (((0,), (0,)), ((), ())),
                preferred_element_type=F32,
            ).astype(BF16)
        for k in range(BLOCKS):
            hits = [(src[0, g * STEP + l] == k).astype(F32) for l in range(STEP)]
            for n in range(4):
                rows = pl.ds(n * 32, 32)
                total = extra[k, rows, :]
                for l in range(STEP):
                    total = total + hits[l] * part[l, rows, :].astype(F32)
                extra[k, rows, :] = total
        return 0

    lax.fori_loop(0, local_slots // STEP, local_group, 0)
    total = jnp.zeros((WIDTH, WIDTH), F32)
    for t in range(BLOCKS):
        self_out[t] = jnp.dot(feats_here[t], self_weight[...], preferred_element_type=F32)
        total += lax.dot_general(feats_here[t], cot[t], (((0,), (0,)), ((), ())), preferred_element_type=F32)
    self_grad[...] = total
    slot_chunk(CHUNKS - 2).wait()
    slot_chunk(CHUNKS - 1).wait()
    for copy in list(first.values()) + list(second.values()):
        copy.wait_send()
    free(3)
    free(2)
    for group in range(SIDE):
        for copy in lines[group][:21]:
            copy.wait_recv()


def spread_features(coeffs, slots, feats, picks, bases, scaled, cot, self_weight, remote_adj, local_adj):
    relations, remote_slots = coeffs.shape[0], remote_adj.shape[0]
    dma = pltpu.SemaphoreType.DMA
    return pl.pallas_call(
        spread_kernel,
        out_shape=[jax.ShapeDtypeStruct((SIDE, CORES, SIDE, SIDE, 2, ROWS, WIDTH), BF16)]
        + [jax.ShapeDtypeStruct((SIDE, SIDE) + picks.shape, jnp.int32)] * 3
        + [
            jax.ShapeDtypeStruct((relations, WIDTH, WIDTH), BF16),
            jax.ShapeDtypeStruct((BLOCKS, ROWS, WIDTH), F32),
            jax.ShapeDtypeStruct((remote_slots, ROWS, WIDTH), BF16),
            jax.ShapeDtypeStruct((BLOCKS, ROWS, WIDTH), F32),
            jax.ShapeDtypeStruct((WIDTH, WIDTH), F32),
        ],
        in_specs=[SMEM] * 7 + [ANY] * 2 + [VMEM] * 4 + [ANY] * 2,
        out_specs=[ANY] * 4 + [VMEM] * 2 + [ANY] + [VMEM] * 2,
        scratch_shapes=[pltpu.VMEM((BLOCKS, ROWS, WIDTH), BF16)]
        + [pltpu.VMEM((SIDE, BLOCKS, rows, WIDTH), BF16) for *_, rows in PARTS for _ in range(SIDE)]
        + [pltpu.SMEM((SIDE, SIDE) + picks.shape, jnp.int32)] * 3
        + [pltpu.VMEM((2, 8, SIDE, 2, rows, WIDTH), BF16) for *_, rows in PARTS]
        + [
            pltpu.VMEM(remote_adj.shape, BF16),
            pltpu.VMEM(local_adj.shape, BF16),
            pltpu.VMEM((relations, BLOCKS, ROWS, WIDTH), BF16),
            pltpu.VMEM((2, remote_slots // CHUNKS, ROWS, WIDTH), BF16),
            pltpu.VMEM((STEP, ROWS, WIDTH), BF16),
            dma((3, 2)), dma((3,)), dma((CHUNKS,)),
            dma((3, 3)), dma((3, 3)), dma((3, 3)), dma((3, 3)), dma((3,)),
            dma((3, 2, 2)), dma((3, 2, 2)), dma((3, SIDE, 2, 2)), dma((3, SIDE, 2, 2)),
            dma((3, 7, SIDE)), dma((3, 7, SIDE)), dma((3, SIDE)),
        ],
        compiler_params=pltpu.CompilerParams(collective_id=0, has_side_effects=True, vmem_limit_bytes=58 * MIB),
        name="spread_features",
    )(coeffs, *slots, feats, picks, bases, scaled, cot, self_weight, remote_adj, local_adj)


def return_kernel(
    coeffs, i0, i1, i2, grads, extra, outer_in, bases_in, self_grad, out, full, rest,
    r0, r1, r2, p0, p1, p2, l0, l1, l2, e0, e1, e2, q0, q1, q2, f0, f1, f2, added, outer, bases, inner, terms,
    wire, b0, b1, h1, b2, h2, b3, total,
    send, recv, own_sem, es, ev, ls, lv, s2, v2, pair_sem, ws, wr,
):
    me = place()
    ids, returned, sums, landed = (i0, i1, i2), (r0, r1, r2), (p0, p1, p2), (l0, l1, l2)
    early, held, final = (e0, e1, e2), (q0, q1, q2), (f0, f1, f2)
    core, partner = me["c"], {**me, "c": (me["c"] + 1) % CORES}
    relations, basis_count = coeffs.shape
    own = [
        pltpu.make_async_copy(outer_in, outer, own_sem.at[3]),
        pltpu.make_async_copy(bases_in, bases, own_sem.at[4]),
        pltpu.make_async_copy(self_grad, terms.at[2, 0, pl.ds(0, 2)], own_sem.at[5]),
        pltpu.make_async_copy(extra, added, own_sem.at[6]),
    ]
    for j, (a1, a2, last, row, rows) in enumerate(PARTS):
        own.append(
            pltpu.make_async_copy(
                band_at(grads, core, row, rows, **{last: me[last]}), returned[j].at[core, me[last]], own_sem.at[j]
            )
        )
    for copy in own:
        copy.start()
    greet([p for axis in AXES for hop, flip, p in line_peers(me, axis) if hop] + [partner])
    sent = [[], [], [], []]

    def give(group):
        for n in range(7):
            for j, (a1, a2, last, row, rows) in enumerate(PARTS):
                hop, flip, peer = line_peers(me, last)[n]
                far = (me[a2] + group) % SIDE
                copy = remote(
                    band_at(grads, peer["c"], row, rows, **{last: peer[last], a2: far}),
                    plane_at(returned[j].at[core, me[last]], last, **{a2: far}),
                    send.at[j, n, group],
                    recv.at[j, n, group],
                    peer,
                )
                copy.start()
                sent[group].append(copy)

    def weigh(stage, level, src, dst):
        copies = []
        for hop in HOPS:
            for j, part in enumerate(PARTS):
                axis = part[level]
                copy = remote(
                    src(j, (me[axis] + hop) % SIDE),
                    dst(j, hop - 1),
                    ws.at[stage, j, hop - 1],
                    wr.at[stage, j, hop - 1],
                    moved(me, axis, hop),
                )
                copy.start()
                copies.append(copy)
        return copies

    def done(copies):
        for copy in copies:
            copy.wait()

    def weight_terms():
        terms[2, 0, 2:4] = jnp.zeros((2, SIDE, SIDE, TERM_ROWS, WIDTH), F32)
        terms[2, 1] = jnp.zeros((SIDE, SIDE, SIDE, TERM_ROWS, WIDTH), F32)
        done(own[:3])

        def mix(n, _):
            for half in range(2):
                totals = [jnp.zeros((32, WIDTH), F32)] * 4
                for r in range(relations):
                    slab = outer[r, pl.ds(n * 32, 32), :]
                    totals = [totals[b] + coeffs[r, half * 4 + b] * slab for b in range(4)]
                for b in range(4):
                    terms[half, b // 2, (b % 2) * 2 + n // 4, n % 4] = totals[b].reshape(4, TERM_ROWS, WIDTH)
            return 0

        lax.fori_loop(0, WIDTH // 32, mix, 0)
        inner[...] = jnp.zeros_like(inner)

        def products(n, _):
            rows = pl.ds(n * 16, 16)
            slabs = [bases[b, rows, :].astype(F32) for b in range(basis_count)]
            for r in range(relations):
                slab = outer[r, rows, :]
                for b in range(basis_count):
                    both = slab * slabs[b]
                    both = both[:8] + both[8:]
                    inner[r * basis_count + b] += both[:, :ROWS] + both[:, ROWS:]
            return 0

        lax.fori_loop(0, WIDTH // 16, products, 0)
        for r in range(relations):
            terms[2, 0, 2 + r // 16, (r // 4) % 4, r % 4, :, pl.ds(0, ROWS)] = jnp.sum(
                inner[pl.ds(r * basis_count, basis_count)], axis=1
            )

    def piece(j, depth):
        spot = tuple(me[PARTS[j][level]] for level in (2, 1, 0)[:depth])
        return total.at[(j, core) + spot]

    def add(*parts):
        return sum(part.astype(F32) for part in parts[1:]) + parts[0].astype(F32)

    def spot_of(j, group, k):
        a1, a2, last, row, rows = PARTS[j]
        where = {a1: k, a2: (me[a2] + group) % SIDE}
        return tuple(where[a] for a in plane_dims(last))

    def fold(j, group, k, low, high, way=None):
        a1, a2, last, row, rows = PARTS[j]
        spot = spot_of(j, group, k)

        def two(n, _):
            if way is None:
                totals = [jnp.zeros((rows, WIDTH), F32)] * 2
            else:
                totals = [early[j][way, k, 2 * n + h - low].astype(F32) for h in range(2)]
            for other in range(CORES):
                for place_on in range(SIDE):
                    owner = band({**me, "c": other, last: place_on})
                    for c in range(2):
                        block = ids[j][spot + (c, owner)]
                        grad = returned[j][(other, place_on) + spot + (c,)].astype(F32)
                        totals = [totals[h] + (block == 2 * n + h).astype(F32) * grad for h in range(2)]
            for h in range(2):
                sums[j][spot + (2 * n + h,)] = totals[h].astype(BF16)
            return 0

        lax.fori_loop(low // 2, high // 2, two, 0)

    def half_on(j, way, k):
        return remote(
            sums[j].at[spot_of(j, 2, k) + (pl.ds(way * 4, 4),)], early[j].at[way, k], es.at[j, way, k],
            ev.at[j, way, k], moved(me, PARTS[j][1], (1, 3)[way]),
        )

    def across(j, way, late, k):
        low = 4 * way if late else 4 - 4 * way
        return remote(
            sums[j].at[spot_of(j, (1, 3)[way], k) + (pl.ds(low, 4),)], landed[j].at[way, k, pl.ds(low, 4)],
            ls.at[j, way, late, k], lv.at[j, way, late, k], moved(me, PARTS[j][1], (1, 3)[way]),
        )

    def each_band(work):
        def one(k, _):
            for j in range(3):
                work(j, k)
            return 0

        lax.fori_loop(0, SIDE, one, 0)

    def far_bands(j, k):
        fold(j, 2, k, 0, BLOCKS)
        half_on(j, 0, k).start()
        half_on(j, 1, k).start()

    def near_bands(way, late):
        def work(j, k):
            low = 4 * way if late else 4 - 4 * way
            if late:
                half_on(j, way, k).wait()
            fold(j, (1, 3)[way], k, low, low + 4, way if late else None)
            across(j, way, late, k).start()

        return work

    give(2)
    give(1)
    weight_terms()
    for j in range(3):
        for c in range(CORES):
            for k in range(SIDE):
                slab = terms[j, c, k]
                wire[j, c, k] = jnp.concatenate([slab[..., :ROWS], slab[..., ROWS:]], axis=2).astype(BF16)
    halves = remote(wire.at[:, partner["c"]], b0, pair_sem.at[0], pair_sem.at[1], partner)
    halves.start()
    done(own[3:])
    halves.wait()
    b0[...] = add(wire[:, core], b0[...]).astype(BF16)
    stage = weigh(0, 2, lambda j, k: b0.at[j, k], lambda j, h: b1.at[j, h])
    give(3)
    done(sent[2])
    done(stage)
    for j, part in enumerate(PARTS):
        h1[j] = add(b0[j, me[part[2]]], b1[j, 0], b1[j, 1], b1[j, 2]).astype(BF16)
    stage = weigh(1, 1, lambda j, k: h1.at[j, k], lambda j, h: b2.at[j, h])
    each_band(far_bands)
    done(stage)
    for j, part in enumerate(PARTS):
        h2[j] = add(h1[j, me[part[1]]], b2[j, 0], b2[j, 1], b2[j, 2]).astype(BF16)
    stage = weigh(2, 0, lambda j, k: h2.at[j, k], lambda j, h: b3.at[j, h])
    done(stage)
    for j, part in enumerate(PARTS):
        piece(j, 3)[...] = add(h2[j, me[part[0]]], b3[j, 0], b3[j, 1], b3[j, 2]).astype(BF16)
    stage = weigh(3, 0, lambda j, k: piece(j, 3), lambda j, h: piece(j, 3))
    give(0)
    done(sent[1])
    each_band(near_bands(0, 0))
    done(stage)
    stage = weigh(4, 1, lambda j, k: piece(j, 2), lambda j, h: piece(j, 2))
    done(sent[3])
    each_band(near_bands(1, 0))
    done(stage)
    stage = weigh(5, 2, lambda j, k: piece(j, 1), lambda j, h: piece(j, 1))
    each_band(near_bands(0, 1))
    each_band(near_bands(1, 1))
    done(sent[0])
    each_band(lambda j, k: fold(j, 0, k, 0, BLOCKS))
    done(stage)
    back = remote(total.at[:, core], total.at[:, core], pair_sem.at[2], pair_sem.at[3], partner)
    back.start()
    for j in range(3):
        for way in range(2):
            for late in range(2):
                for k in range(SIDE):
                    across(j, way, late, k).wait()
    second = []
    for hop in HOPS + (0,):
        for j, (a1, a2, last, row, rows) in enumerate(PARTS):
            k = (me[a1] + hop) % SIDE
            mine = sums[j].at[spot_of(j, 0, k)]

            def join(n, _, j=j, k=k, hop=hop, mine=mine):
                both = mine[n].astype(F32) + landed[j][0, k, n].astype(F32) + landed[j][1, k, n].astype(F32)
                held[j][hop, n] = both.astype(BF16)
                return 0

            lax.fori_loop(0, BLOCKS, join, 0)
            if hop:
                copy = remote(
                    held[j].at[hop], final[j].at[hop - 1], s2.at[j, hop - 1], v2.at[j, hop - 1], moved(me, a1, hop)
                )
                copy.start()
                second.append(copy)
    done(second)
    for j, (a1, a2, last, row, rows) in enumerate(PARTS):

        def end(n, _, j=j, row=row, rows=rows):
            both = added[n, pl.ds(row, rows), :] + held[j][0, n].astype(F32)
            for h in range(3):
                both = both + final[j][h, n].astype(F32)
            out[n, pl.ds(row, rows), :] = both.astype(BF16)
            return 0

        lax.fori_loop(0, BLOCKS, end, 0)
    back.wait()
    for j in range(3):
        ref = full.at[j] if j < 2 else rest.at[0]
        for c in range(CORES):
            for k in range(SIDE):
                slab = total[j, c, k].astype(F32)
                ref[c, k, :, :, :, pl.ds(0, ROWS)] = slab[:, :, :TERM_ROWS]
                ref[c, k, :, :, :, pl.ds(ROWS, ROWS)] = slab[:, :, TERM_ROWS:]


def return_grads(coeffs, ids, grads, extra, outer, bases, self_grad):
    dma = pltpu.SemaphoreType.DMA
    piece, packed = (TERM_ROWS, WIDTH), (2 * TERM_ROWS, ROWS)
    relations, basis_count = coeffs.shape
    return pl.pallas_call(
        return_kernel,
        out_shape=[
            jax.ShapeDtypeStruct((BLOCKS, ROWS, WIDTH), BF16),
            jax.ShapeDtypeStruct((2, CORES, SIDE, SIDE, SIDE) + piece, F32),
            jax.ShapeDtypeStruct((1, CORES, SIDE, SIDE, SIDE) + piece, F32),
        ],
        in_specs=[SMEM] * 4 + [ANY] * 5,
        out_specs=[VMEM] * 3,
        scratch_shapes=[pltpu.VMEM((CORES, SIDE, SIDE, SIDE, 2, rows, WIDTH), BF16) for *_, rows in PARTS]
        + [pltpu.VMEM((SIDE, SIDE, BLOCKS, rows, WIDTH), BF16) for *_, rows in PARTS]
        + [pltpu.VMEM((2, SIDE, BLOCKS, rows, WIDTH), BF16) for *_, rows in PARTS]
        + [pltpu.VMEM((2, SIDE, BLOCKS // 2, rows, WIDTH), BF16) for *_, rows in PARTS]
        + [pltpu.VMEM((SIDE, BLOCKS, rows, WIDTH), BF16) for *_, rows in PARTS]
        + [pltpu.VMEM((3, BLOCKS, rows, WIDTH), BF16) for *_, rows in PARTS]
        + [
            pltpu.VMEM((BLOCKS, ROWS, WIDTH), F32),
            pltpu.VMEM(outer.shape, F32),
            pltpu.VMEM(bases.shape, BF16),
            pltpu.VMEM((relations * basis_count, 8, ROWS), F32),
            pltpu.VMEM((3, CORES, SIDE, SIDE, SIDE) + piece, F32),
            pltpu.VMEM((3, CORES, SIDE, SIDE, SIDE) + packed, BF16),
            pltpu.VMEM((3, SIDE, SIDE, SIDE) + packed, BF16),
            pltpu.VMEM((3, 3, SIDE, SIDE) + packed, BF16),
            pltpu.VMEM((3, SIDE, SIDE) + packed, BF16),
            pltpu.VMEM((3, 3, SIDE) + packed, BF16),
            pltpu.VMEM((3, SIDE) + packed, BF16),
            pltpu.VMEM((3, 3) + packed, BF16),
            pltpu.VMEM((3, CORES, SIDE, SIDE, SIDE) + packed, BF16),
            dma((3, 7, SIDE)), dma((3, 7, SIDE)), dma((7,)),
            dma((3, 2, SIDE)), dma((3, 2, SIDE)), dma((3, 2, 2, SIDE)), dma((3, 2, 2, SIDE)), dma((3, 3)), dma((3, 3)),
            dma((6,)), dma((6, 3, 3)), dma((6, 3, 3)),
        ],
        compiler_params=pltpu.CompilerParams(collective_id=2, has_side_effects=True, vmem_limit_bytes=60 * MIB),
        name="return_grads",
    )(coeffs, *ids, grads, extra, outer, bases, self_grad)


def piece_specs(steps, start, width):
    size = WIDE // PIECES

    def at(q):
        return lambda i: (jnp.clip(i - start, 0, steps - 1) * PIECES + q, 0, 0)

    return [
        pl.BlockSpec((size, ROWS, width), at(q)) for q in range(PIECES)
    ]


def slot_specs(remote_steps, local_steps):
    return piece_specs(remote_steps, 0, ROWS) + piece_specs(local_steps, remote_steps, ROWS)


def slot_of(pieces, l):
    return pieces[l // (WIDE // PIECES)][l % (WIDE // PIECES)]


def whole(shape):
    return pl.BlockSpec(shape, lambda i: (0,) * len(shape), pipeline_mode=pl.Buffered(1))


def slot_ids(remote, i, l, recv_tgt, recv_rel, recv_count, local_tgt, local_rel):
    if remote:
        peer, c = i * (WIDE // 2) + l // 2, l % 2
        return recv_tgt[c, peer], recv_rel[c, peer], (c < recv_count[0, peer]).astype(F32)
    return local_tgt[0, i * WIDE + l], local_rel[0, i * WIDE + l], 1.0


def degree_kernel(
    recv_tgt, recv_rel, recv_count, local_tgt, local_rel, src, remote_adj, local_adj, cot, scaled, norm,
    total, remote_here, local_here, sem,
):
    lists = (recv_tgt, recv_rel, recv_count, local_tgt, local_rel)
    pairs = ((remote_adj, remote_here), (local_adj, local_here))
    copies = []
    for from_, to in pairs:
        for n in range(from_.shape[0] // WIDE):
            part = pl.ds(n * WIDE, WIDE)
            copies.append(pltpu.make_async_copy(from_.at[part], to.at[part], sem.at[len(copies)]))
            copies[-1].start()
    total[...] = jnp.zeros_like(total)
    done = 0
    for remote_side, (from_, to) in enumerate(pairs):
        for n in range(from_.shape[0] // WIDE):
            copies[done].wait()
            done += 1
            for l in range(WIDE):
                t, r, valid = slot_ids(remote_side == 0, n, l, *lists)
                total[t] += to[n * WIDE + l].astype(F32) * valid
    for t in range(BLOCKS):
        row_norm = lax.rsqrt(1.0 + jnp.sum(total[t], axis=1, keepdims=True))
        scaled[t] = (cot[t].astype(F32) * row_norm).astype(BF16)
        norm[t] = jnp.broadcast_to(row_norm, (ROWS, ROWS))


def degrees(slots, remote_adj, local_adj, cot):
    parts = (remote_adj.shape[0] + local_adj.shape[0]) // WIDE
    return pl.pallas_call(
        degree_kernel,
        out_shape=[
            jax.ShapeDtypeStruct((BLOCKS, ROWS, WIDTH), BF16),
            jax.ShapeDtypeStruct((BLOCKS, ROWS, ROWS), F32),
        ],
        in_specs=[SMEM] * 6 + [ANY] * 2 + [VMEM],
        out_specs=[VMEM] * 2,
        scratch_shapes=[
            pltpu.VMEM((BLOCKS, ROWS, ROWS), F32),
            pltpu.VMEM(remote_adj.shape, BF16),
            pltpu.VMEM(local_adj.shape, BF16),
            pltpu.SemaphoreType.DMA((parts,)),
        ],
        compiler_params=pltpu.CompilerParams(vmem_limit_bytes=58 * MIB),
        name="degrees",
    )(*slots, remote_adj, local_adj, cot)


def forward_kernel(
    remote_steps, recv_tgt, recv_rel, recv_count, local_tgt, local_rel, src, *refs,
):
    remote_adj, local_adj, incoming = (refs[n * PIECES : (n + 1) * PIECES] for n in range(3))
    feats, weights, scaled, norm, self_out, out, outer, mixed, held = refs[3 * PIECES :]
    i = pl.program_id(0)
    lists = (recv_tgt, recv_rel, recv_count, local_tgt, local_rel)

    @pl.when(i == 0)
    def _():
        mixed[...] = jnp.zeros_like(mixed)
        outer[...] = jnp.zeros_like(outer)

    def visit(remote, step, adj, rows_of):
        for l in range(WIDE):
            t, r, valid = slot_ids(remote, step, l, *lists)
            held[l] = (jnp.dot(slot_of(adj, l), rows_of(l), preferred_element_type=F32) * valid).astype(BF16)
        for l in range(WIDE):
            t, r, valid = slot_ids(remote, step, l, *lists)
            mixed[t] += jnp.dot(held[l], weights[r], preferred_element_type=F32)
            outer[r] += lax.dot_general(held[l], scaled[t], (((0,), (0,)), ((), ())), preferred_element_type=F32)

    @pl.when(i < remote_steps)
    def _():
        visit(True, i, remote_adj, lambda l: slot_of(incoming, l))

    @pl.when(i >= remote_steps)
    def _():
        step = i - remote_steps
        visit(False, step, local_adj, lambda l: feats[src[0, step * WIDE + l]])

    @pl.when(i == pl.num_programs(0) - 1)
    def _():
        for t in range(BLOCKS):
            for half in range(2):
                cols = pl.ds(half * ROWS, ROWS)
                out[t, :, cols] = (norm[t] * mixed[t, :, cols] + self_out[t, :, cols]).astype(BF16)


def forward_slots(slots, remote_adj, local_adj, incoming, feats, weights, scaled, norm, self_out):
    remote_steps, local_steps = remote_adj.shape[0] // WIDE, local_adj.shape[0] // WIDE
    relations = weights.shape[0]
    return pl.pallas_call(
        functools.partial(forward_kernel, remote_steps),
        grid=(remote_steps + local_steps,),
        out_shape=[
            jax.ShapeDtypeStruct((BLOCKS, ROWS, WIDTH), BF16),
            jax.ShapeDtypeStruct((relations, WIDTH, WIDTH), F32),
        ],
        in_specs=[SMEM] * 6
        + slot_specs(remote_steps, local_steps)
        + piece_specs(remote_steps, 0, WIDTH)
        + [whole(a.shape) for a in (feats, weights, scaled, norm, self_out)],
        out_specs=[whole((BLOCKS, ROWS, WIDTH)), whole((relations, WIDTH, WIDTH))],
        scratch_shapes=[pltpu.VMEM((BLOCKS, ROWS, WIDTH), F32), pltpu.VMEM((WIDE, ROWS, WIDTH), BF16)],
        compiler_params=pltpu.CompilerParams(vmem_limit_bytes=58 * MIB),
        name="forward_slots",
    )(
        *slots, *[remote_adj] * PIECES, *[local_adj] * PIECES, *[incoming] * PIECES, feats, weights, scaled, norm,
        self_out,
    )


def local(
    node_feats, send_block, recv_block, recv_rel, recv_count, recv_adj, local_src, local_tgt, local_rel, local_adj,
    bases, coeffs, self_weight, cotangent,
):
    peers = lax.axis_size(("src", "tgt"))
    slot_cap = send_block.shape[2]
    remote_slots = peers * slot_cap
    relations, basis_count = coeffs.shape
    feats = node_feats.reshape(BLOCKS, ROWS, WIDTH)
    cot = cotangent.reshape(BLOCKS, ROWS, WIDTH)
    remote_adj = recv_adj.reshape(remote_slots, ROWS, ROWS)
    own_adj = local_adj[0]
    slots = (recv_block[0].T, recv_rel[0].T, recv_count, local_tgt, local_rel, local_src)
    wide_coeffs = coeffs.astype(F32)
    scaled, norm = degrees(slots, remote_adj, own_adj, cot)
    incoming, *ids, weights, extra, grads, self_out, self_grad = spread_features(
        wide_coeffs, slots, feats, send_block[0].T, bases, scaled, cot, self_weight, remote_adj, own_adj
    )
    incoming = incoming.reshape(remote_slots, ROWS, WIDTH)
    features_out, outer = forward_slots(slots, remote_adj, own_adj, incoming, feats, weights, scaled, norm, self_out)
    grad_features, grad_bases, rest = return_grads(
        wide_coeffs,
        ids,
        grads.reshape(SIDE, CORES, SIDE, SIDE, slot_cap, ROWS, WIDTH),
        extra,
        outer,
        bases,
        self_grad.reshape(2, SIDE, SIDE, TERM_ROWS, WIDTH),
    )
    scale = 1.0 / math.sqrt(node_feats.shape[0] * peers)
    rest = rest.reshape(-1, WIDTH)
    coef = rest[WIDTH : WIDTH + relations * basis_count, :ROWS]
    return (
        features_out.reshape(node_feats.shape),
        grad_features.reshape(node_feats.shape),
        grad_bases.reshape(bases.shape) * scale,
        jnp.sum(coef, axis=1).reshape(relations, basis_count) * scale,
        rest[:WIDTH] * scale,
    )


def solution(mesh):
    both = ("src", "tgt")
    in_specs = (
        P(both, None),
        P(both, None, None),
        P(both, None, None),
        P(both, None, None),
        P(both, None),
        P(both, None, None, None, None),
        P(both, None),
        P(both, None),
        P(both, None),
        P(both, None, None, None),
        P(),
        P(),
        P(),
        P(both, None),
    )
    out_specs = (P(both, None), P(both, None), P(), P(), P())
    return jax.shard_map(local, mesh=mesh, in_specs=in_specs, out_specs=out_specs, check_vma=False)
```
